256 devices in a mesh: grp: 16 (over y_lo, z), mem: 16 (over y_hi, x, core).
Axes of the slice: x: 4, y: 4 (y_hi: 2, y_lo: 2; y = y_hi * 2 + y_lo), z: 8, core: 2. Of those that a mesh axis runs over, the one named last changes fastest.
Arguments:
- obs_resid: float32 [131072, 64], P(('grp', 'mem')), may hold values from -6 to 6
- weight: float32 [131072, 64], P(('grp', 'mem')), may hold values from 0.1 to 10
- jac_src: float32 [5, 131072, 64], P(None, ('grp', 'mem')), may hold values from -6 to 6
- att_part: float32 [4, 131072, 64], P(None, ('grp', 'mem')), may hold values from -6 to 6
- seg_index: int32 [131072, 64], P(('grp', 'mem')), may hold values from 0 to 1023
- jac_cal: bfloat16 [131072, 64, 64], P(('grp', 'mem')), may hold values from -6 to 6
- cal_index: int32 [131072], P(('grp', 'mem')), may hold values from 0 to 16383, as said below
- block_count: int32 [256], P(('grp', 'mem')), may hold values from 1 to 512, 81920 in all
Outputs:
- src_update: float32 [5, 131072], P(None, ('grp', 'mem'))
- att_update: float32 [4, 1024], P(None, 'mem')
- cal_update: float32 [16384, 64], P(('grp', 'mem'))
- new_resid: float32 [131072, 64], P(('grp', 'mem'))
The draws below stay inside these ranges and needn't reach their ends.
Inputs may be any that keep to these rules, and one draw needn't show every extreme that they name: `cal_index`: of the 512 source slots of one device, at most 4 have calibration blocks c with the same c // 64; some such share receives exactly 4 from every device.
All inputs are finite; a program needn't handle non-finite values. No bound on the sum of `block_count` on one device may be relied on, other than what follows from the above.
Results may differ from the reference program's by a relative error of at most 0.0003.
Values sent between devices are 32-bit elements; how exact they have to be, the bound alone decides.
No kernel may reach another device: no remote copies, remote signals or barrier semaphores. Data moves between devices by JAX's collectives and lax.ppermute only.
A program may use at most 64 MiB of HBM per device.

```python
import math
import jax
import jax.numpy as jnp
import numpy as np
from jax import lax

CALB = 16384
CPAR = 64
KNOTS = 1024
OBS = 64
BLK_DEV = 512
DEVICE_TOTAL = 256
SOURCES = 131072
SLOT_LIMIT = 4


def draw_cal_index(key, part):
    key = jax.random.fold_in(key, 7)
    key_owner, key_slots, key_rows, key_offset = jax.random.split(key, 4)
    slot_number = DEVICE_TOTAL * SLOT_LIMIT
    share = CALB // DEVICE_TOTAL
    picked_holder = jax.random.randint(key_owner, (), 0, DEVICE_TOTAL).astype(jnp.int32)
    key_per_slot = jax.random.split(key_slots, DEVICE_TOTAL)
    owner_scores = jax.vmap(lambda slot_rank: jax.random.permutation(slot_rank, slot_number).astype(jnp.int32))(key_per_slot)
    holder_of_slot = (jnp.arange(slot_number, dtype=jnp.int32) // SLOT_LIMIT)[None, :]
    owner_scores = owner_scores - jnp.where(holder_of_slot == picked_holder, slot_number, 0).astype(jnp.int32)
    order = jnp.argsort(owner_scores, axis=1).astype(jnp.int32)
    owners = order[:, :BLK_DEV] // SLOT_LIMIT
    row_keys = jax.random.split(key_rows, DEVICE_TOTAL)
    row_order = jax.vmap(lambda slot_rank: jax.random.permutation(slot_rank, BLK_DEV).astype(jnp.int32))(row_keys)
    owners = jnp.take_along_axis(owners, row_order, axis=1)
    offsets = jax.random.randint(key_offset, (DEVICE_TOTAL, BLK_DEV), 0, share).astype(jnp.int32)
    return (owners * share + offsets).reshape(SOURCES).astype(jnp.int32)


def touch_ends(array, stream_key, smallest, high):
    place = [jax.random.randint(jax.random.fold_in(stream_key, axis), (), 0, length) for axis, length in enumerate(array.shape)]
    longest = array.shape.index(max(array.shape))
    neighbour = place[:longest] + [(place[longest] + 1) % array.shape[longest]] + place[longest + 1:]
    return array.at[tuple(place)].set(smallest).at[tuple(neighbour)].set(high)


def block_scale(stream_key, dims, shards, least, high):
    level = 1.0
    for axis_at, blocks in shards:
        draws = jax.random.uniform(jax.random.fold_in(jax.random.fold_in(stream_key, 6), axis_at), (blocks,), jnp.float32, least / len(shards), high / len(shards))
        level = level * jnp.repeat(jnp.exp(draws), dims[axis_at] // blocks).reshape((-1,) + (1,) * (len(dims) - 1 - axis_at))
    return level


def split_up(count, total, most, skew):
    loads = [(1 << 20) // math.isqrt(standing ** skew) + 1 for standing in range(2, count + 1)]
    spare, counts = total - most - (count - 1), [1] * (count - 1)
    while spare > 0:
        candidates = [i for i in range(count - 1) if counts[i] < most]
        mass, left = sum([loads[i] for i in candidates]), spare
        for i in candidates:
            extra = min(most - counts[i], max(1, left * loads[i] // mass), spare)
            counts[i] = counts[i] + extra
            spare = spare - extra
    return np.array([most] + counts)


def ragged_sizes(rng, count, total, bound, slope):
    if count == 2:
        one = jax.random.randint(rng, (), max(1, total - bound), min(bound, total - 1) + 1)
        return jnp.stack([one, total - one])
    tallies = jnp.asarray(split_up(count, total, bound, slope), jnp.int32)
    couples = (count - 1) // 2
    giver, taker = tallies[1:1 + 2 * couples:2], tallies[2:2 + 2 * couples:2]
    room = jnp.minimum(giver - 1, bound - taker)
    shifted = jax.random.randint(jax.random.fold_in(rng, 1), (couples,), 0, 1 << 20) % (room + 1)
    tallies = tallies.at[1:1 + 2 * couples:2].set(giver - shifted).at[2:2 + 2 * couples:2].set(taker + shifted)
    return tallies[jax.random.permutation(jax.random.fold_in(rng, 2), count)]


def centred(rng, shape, deviation, most, cuts=(), held_as=jnp.bfloat16):
    level = block_scale(rng, shape, cuts, -0.22, 0.18) if cuts else 1.0
    values = jax.random.normal(rng, shape, jnp.float32) * deviation * level
    return jnp.minimum(jnp.maximum(values, -most), most).astype(held_as)


def setup_inputs(seed: int = 0) -> dict:
    streams_of = jax.random.split(jax.random.key(seed), 9)
    return {
        "obs_resid": centred(streams_of[0], (SOURCES, OBS), 1.0, 6.0, ((0, 256),), jnp.float32),
        "weight": jnp.clip(jnp.exp(math.log(10.0) - 4.6051702 * jax.random.uniform(streams_of[1], (SOURCES, OBS), jnp.float32) ** block_scale(streams_of[1], (SOURCES, OBS), ((0, 256),), -0.2, 0.2)), 0.1, 10.0),
        "jac_src": centred(streams_of[2], (5, SOURCES, OBS), 1.0, 6.0, ((1, 256),), jnp.float32),
        "att_part": centred(streams_of[3], (4, SOURCES, OBS), 1.0, 6.0, ((1, 256),), jnp.float32),
        "seg_index": touch_ends(jax.random.randint(streams_of[4], (SOURCES, OBS), 0, KNOTS), jax.random.fold_in(streams_of[4], 1), 0, KNOTS - 1).astype(jnp.int32),
        "jac_cal": centred(streams_of[5], (SOURCES, OBS, CPAR), 1.0, 6.0, ((0, 256),)),
        "cal_index": draw_cal_index(jax.random.fold_in(streams_of[8], 71), 0),
        "block_count": ragged_sizes(streams_of[7], DEVICE_TOTAL, DEVICE_TOTAL * BLK_DEV * 5 // 8, BLK_DEV, 1).astype(jnp.int32),
    }


def reference(obs_resid, weight, jac_src, att_part, seg_index, jac_cal, cal_index, block_count):
    slots = jnp.arange(SOURCES, dtype=jnp.int32)
    owner = slots // BLK_DEV
    used = (slots % BLK_DEV) < block_count[owner]
    live = weight * used.astype(jnp.float32)[:, None]
    numer = jnp.sum(jac_src * (live * obs_resid)[None], axis=2)
    denom = 1.0 + jnp.sum(jac_src * jac_src * live[None], axis=2)
    src_update = numer / denom
    resid_one = obs_resid - jnp.sum(jac_src * src_update[:, :, None], axis=0)
    flat_seg = seg_index.reshape(-1)
    parts = att_part.reshape(4, -1)
    flat_live = live.reshape(-1)
    terms = jnp.concatenate([parts * (flat_live * resid_one.reshape(-1))[None], parts * parts * flat_live[None]], axis=0)
    sums = jax.ops.segment_sum(terms.T, flat_seg, num_segments=KNOTS).T
    att_update = sums[:4] / (1.0 + sums[4:])
    looked = att_update[:, flat_seg]
    new_resid = resid_one - jnp.sum(parts * looked, axis=0).reshape(SOURCES, OBS)
    vec = (live * new_resid).reshape(-1, BLK_DEV, OBS)
    wts = live.reshape(-1, BLK_DEV, OBS)
    blocks = jac_cal.reshape(-1, BLK_DEV, OBS, CPAR)

    def one_device(items):
        jac_block, vec_block, wt_block = items
        jac_f = jac_block.astype(jnp.float32)
        grad = jnp.einsum("brp,br->bp", jac_f, vec_block, precision=lax.Precision.HIGHEST)
        diag = jnp.einsum("brp,br->bp", jac_f * jac_f, wt_block, precision=lax.Precision.HIGHEST)
        return jnp.concatenate([grad, diag], axis=1)

    block_terms = lax.map(one_device, (blocks, vec, wts)).reshape(SOURCES, 2 * CPAR)
    cal_sums = jax.ops.segment_sum(block_terms, cal_index, num_segments=CALB)
    cal_update = cal_sums[:, :CPAR] / (1.0 + cal_sums[:, CPAR:])
    return src_update, att_update, cal_update, new_resid
```

```python
import jax
import jax.numpy as jnp
from jax import lax
from jax.experimental import pallas as pl
from jax.experimental.pallas import tpu as pltpu
from jax.sharding import PartitionSpec as P

CALB = 16384
CPAR = 64
KNOTS = 1024
OBS = 64
SLOTS = 4
AXES = ("grp", "mem")
F32 = jnp.float32
BF16 = jnp.bfloat16
VMEM = pl.BlockSpec(memory_space=pltpu.VMEM)
SMEM = pl.BlockSpec(memory_space=pltpu.SMEM)
ANY = pl.BlockSpec(memory_space=pl.ANY)
LIMIT = pltpu.CompilerParams(vmem_limit_bytes=48 * 1024 * 1024)
NT = (((1,), (1,)), ((), ()))
TN = (((0,), (0,)), ((), ()))


def halves(value):
    top = value.astype(BF16)
    return top, (value - top.astype(F32)).astype(BF16)


def source_kernel(count_ref, obs_ref, wt_ref, js_ref, ap_ref, seg_ref, upd_ref, resid_ref, sums_ref, terms):
    rows, slots = obs_ref.shape
    lane = lax.broadcasted_iota(jnp.int32, (1, slots), 1)
    used = (lane < count_ref[0]).astype(F32)
    live = wt_ref[...] * used
    obs = obs_ref[...]
    weighted = live * obs
    resid = obs
    for k in range(5):
        jac = js_ref[k]
        numer = jnp.sum(jac * weighted, axis=0, keepdims=True)
        denom = 1.0 + jnp.sum(jac * jac * live, axis=0, keepdims=True)
        update = numer / denom
        upd_ref[k : k + 1, :] = update
        resid = resid - jac * update
    resid_ref[...] = resid
    live_resid = live * resid
    for k in range(4):
        part = ap_ref[k]
        grad = part * live_resid
        diag = part * part * live
        for c in range(slots // 128):
            terms[c, pl.ds(k, rows, stride=8), :] = grad[:, 128 * c : 128 * c + 128]
            terms[c, pl.ds(4 + k, rows, stride=8), :] = diag[:, 128 * c : 128 * c + 128]
    ids = lax.broadcasted_iota(jnp.int32, (16, slots), 0).astype(F32).astype(BF16)
    batch = 4

    def step(i, total):
        left, right = [], []
        for b in range(batch):
            r = i * batch + b
            seg = seg_ref[pl.ds(r, 1), :]
            high = jnp.broadcast_to((seg >> 7).astype(F32), (16, slots)).astype(BF16)
            low = jnp.broadcast_to((seg & 127).astype(F32), (16, slots)).astype(BF16)
            place = pl.ds(pl.multiple_of(r * 8, 8), 8)
            value = jnp.concatenate([terms[c, place, :] for c in range(slots // 128)], axis=1)
            top = value.astype(BF16).astype(F32)
            both = jnp.concatenate([value, value - top], axis=0).astype(BF16)
            zero = jnp.zeros_like(both)
            one = jnp.ones_like(both)
            left.append(jnp.concatenate([jnp.where(high == jnp.asarray(h, BF16), both, zero) for h in range(8)], axis=0))
            right.append(jnp.concatenate([jnp.where(low == ids + jnp.asarray(16 * g, BF16), one, zero) for g in range(8)], axis=0))
        return total + lax.dot_general(
            jnp.concatenate(left, axis=1), jnp.concatenate(right, axis=1), NT, preferred_element_type=F32
        )

    total = lax.fori_loop(0, rows // batch, step, jnp.zeros((128, 128), F32))
    for h in range(8):
        sums_ref[8 * h : 8 * h + 8, :] = total[16 * h : 16 * h + 8] + total[16 * h + 8 : 16 * h + 16]


def slot_kernel(row_ref, column_ref, code_ref):
    slots = row_ref.shape[1]
    row = row_ref[...]
    owner = row >> 6
    before = lax.broadcasted_iota(jnp.int32, (slots, slots), 0) < lax.broadcasted_iota(jnp.int32, (slots, slots), 1)
    same = ((column_ref[...] >> 6) == owner) & before
    rank = jnp.sum(same.astype(F32), axis=0, keepdims=True)
    owner_f = owner.astype(F32)
    offset_f = (row & 63).astype(F32)
    for j in range(SLOTS):
        mine = rank == float(j)
        code_ref[j : j + 1, :] = jnp.where(mine, owner_f, -1.0)
        code_ref[SLOTS + j : SLOTS + j + 1, :] = jnp.where(mine, offset_f, 0.0)


def residual_kernel(
    count_ref, sums_ref, wt_ref, ap_ref, seg_ref, resid_ref, code_ref, jac_ref, out_ref, send_ref, jac_buf, vec_buf, live_buf, terms, sem
):
    rows, slots = wt_ref.shape
    copy = pltpu.make_async_copy(jac_ref, jac_buf, sem)
    copy.start()
    lane = lax.broadcasted_iota(jnp.int32, (1, slots), 1)
    used = (lane < count_ref[0]).astype(F32)
    live_buf[...] = wt_ref[...] * used
    tables = []
    for h in range(8):
        tile = sums_ref[8 * h : 8 * h + 8, :]
        tables.append(tile[0:4] / (1.0 + tile[4:8]))

    def look(i, carry):
        base = pl.multiple_of(i * 8, 8)
        for c in range(slots // 128):
            lanes = slice(128 * c, 128 * c + 128)
            seg = seg_ref[pl.ds(base, 8), lanes]
            low = seg & 127
            high = seg >> 7
            new = resid_ref[pl.ds(base, 8), lanes]
            masks = [high == h for h in range(8)]
            for k in range(4):
                found = jnp.zeros((8, 128), F32)
                for h in range(8):
                    table = jnp.broadcast_to(tables[h][k : k + 1, :], (8, 128))
                    found = jnp.where(masks[h], jnp.take_along_axis(table, low, axis=1), found)
                new = new - ap_ref[k, pl.ds(base, 8), lanes] * found
            out_ref[pl.ds(base, 8), lanes] = new
            vec_buf[pl.ds(base, 8), lanes] = new * live_buf[pl.ds(base, 8), lanes]
        return carry

    lax.fori_loop(0, rows // 8, look, 0)
    copy.wait()
    for c in range(slots // 128):
        lanes = slice(128 * c, 128 * c + 128)

        def blocks(i, carry):
            grad, diag = carry
            place = pl.ds(pl.multiple_of(i * 8, 8), 8)
            vec, live = vec_buf[place, lanes], live_buf[place, lanes]
            for b in range(8):
                jac = jac_buf[i * 8 + b, :, lanes].astype(F32)
                grad = grad + jac * vec[b : b + 1]
                diag = diag + jac * jac * live[b : b + 1]
            return grad, diag

        zero = jnp.zeros((CPAR, 128), F32)
        grad, diag = lax.fori_loop(0, rows // 8, blocks, (zero, zero))
        terms[0:CPAR, lanes] = grad
        terms[CPAR : 2 * CPAR, lanes] = diag
    top, rest = halves(terms[...])
    both = jnp.concatenate([top, rest], axis=0)
    owners = send_ref.shape[0]
    ids = lax.broadcasted_iota(jnp.int32, (owners, slots), 0).astype(F32).astype(BF16)
    one = jnp.ones((owners, slots), BF16)
    zero = jnp.zeros((owners, slots), BF16)
    anywhere = zero
    for j in range(SLOTS):
        code = jnp.broadcast_to(code_ref[j : j + 1, :], (owners, slots)).astype(BF16)
        pick = jnp.where(ids == code, one, zero)
        anywhere = anywhere + pick
        moved = lax.dot_general(pick, both, NT, preferred_element_type=F32)
        send_ref[:, 128 * j : 128 * j + 128] = moved[:, 0:128] + moved[:, 128:256]
    offsets = jnp.concatenate([code_ref[SLOTS : 2 * SLOTS, :], jnp.zeros((128 - SLOTS, slots), F32)], axis=0).astype(BF16)
    send_ref[:, 128 * SLOTS : 128 * SLOTS + 128] = lax.dot_general(anywhere, offsets, NT, preferred_element_type=F32)


def gather_kernel(got_ref, out_ref):
    devices = got_ref.shape[0]
    ids = lax.broadcasted_iota(jnp.int32, (devices, 64), 1).astype(F32)
    total = jnp.zeros((64, 256), F32)
    for j in range(SLOTS):
        offset = got_ref[:, 128 * SLOTS + j : 128 * SLOTS + j + 1]
        pick = (ids == offset).astype(F32).astype(BF16)
        top, rest = halves(got_ref[:, 128 * j : 128 * j + 128])
        total = total + lax.dot_general(pick, jnp.concatenate([top, rest], axis=1), TN, preferred_element_type=F32)
    sums = total[:, 0:128] + total[:, 128:256]
    out_ref[...] = sums[:, 0:CPAR] / (1.0 + sums[:, CPAR : 2 * CPAR])


def step_pairs(core, x, y, z):
    pairs = []
    for i in range(256):
        grp, mem = divmod(i, 16)
        c, px, py, pz = mem & 1, (mem >> 1) & 3, ((mem >> 3) << 1) | (grp >> 3), grp & 7
        c, px, py, pz = c ^ core, px ^ x, py ^ y, pz ^ z
        pairs.append((i, ((py & 1) * 8 + pz) * 16 + (py >> 1) * 8 + px * 2 + c))
    return pairs


def sum_everywhere(value):
    for step in ((1, 0, 0, 0), (0, 1, 0, 0), (0, 3, 0, 0), (0, 0, 1, 0), (0, 0, 3, 0), (0, 0, 0, 1), (0, 0, 0, 2), (0, 0, 0, 4)):
        value = value + lax.ppermute(value, AXES, step_pairs(*step))
    return value


def body(obs_resid, weight, jac_src, att_part, seg_index, jac_cal, cal_index, block_count):
    slots = obs_resid.shape[0]
    devices = lax.axis_size(AXES)
    obs, wt, seg = obs_resid.T, weight.T, seg_index.T
    js, ap = jac_src.transpose(0, 2, 1), att_part.transpose(0, 2, 1)
    jac = jac_cal.transpose(1, 2, 0)
    src_update, resid_one, sums = pl.pallas_call(
        source_kernel,
        out_shape=(
            jax.ShapeDtypeStruct((5, slots), F32),
            jax.ShapeDtypeStruct((OBS, slots), F32),
            jax.ShapeDtypeStruct((64, 128), F32),
        ),
        in_specs=[SMEM] + [VMEM] * 5,
        out_specs=(VMEM,) * 3,
        scratch_shapes=[pltpu.VMEM((slots // 128, OBS * 8, 128), F32)],
        compiler_params=LIMIT,
        name="source_step",
    )(block_count, obs, wt, js, ap, seg)
    code = pl.pallas_call(
        slot_kernel,
        out_shape=jax.ShapeDtypeStruct((2 * SLOTS, slots), F32),
        in_specs=[VMEM] * 2,
        out_specs=VMEM,
        compiler_params=LIMIT,
        name="slot_step",
    )(cal_index[None, :], cal_index[:, None])
    total = sum_everywhere(sums)
    new_resid, send = pl.pallas_call(
        residual_kernel,
        out_shape=(jax.ShapeDtypeStruct((OBS, slots), F32), jax.ShapeDtypeStruct((devices, 128 * (SLOTS + 1)), F32)),
        in_specs=[SMEM] + [VMEM] * 6 + [ANY],
        out_specs=(VMEM,) * 2,
        scratch_shapes=[
            pltpu.VMEM((OBS, CPAR, slots), BF16),
            pltpu.VMEM((OBS, slots), F32),
            pltpu.VMEM((OBS, slots), F32),
            pltpu.VMEM((2 * CPAR, slots), F32),
            pltpu.SemaphoreType.DMA,
        ],
        compiler_params=LIMIT,
        name="residual_step",
    )(block_count, total, wt, ap, seg, resid_one, code, jac)
    got = lax.all_to_all(send, AXES, 0, 0, tiled=True)
    cal_update = pl.pallas_call(
        gather_kernel,
        out_shape=jax.ShapeDtypeStruct((CALB // devices, CPAR), F32),
        in_specs=[VMEM],
        out_specs=VMEM,
        compiler_params=LIMIT,
        name="calibration_step",
    )(got)
    table = total.reshape(8, 8, 128)
    table = table[:, 0:4] / (1.0 + table[:, 4:8])
    mem = lax.axis_index("mem")
    att_out = lax.dynamic_slice(table, (mem // 2, 0, (mem % 2) * 64), (1, 4, 64))[0]
    return src_update, att_out, cal_update, new_resid.T


def solution(mesh):
    return jax.shard_map(
        body,
        mesh=mesh,
        in_specs=(
            P(AXES, None),
            P(AXES, None),
            P(None, AXES, None),
            P(None, AXES, None),
            P(AXES, None),
            P(AXES, None, None),
            P(AXES),
            P(AXES),
        ),
        out_specs=(P(None, AXES), P(None, "mem"), P(AXES, None), P(AXES, None)),
        check_vma=False,
    )
```

```python
import jax
import jax.numpy as jnp
from jax import lax
from jax.experimental import pallas as pl
from jax.experimental.pallas import tpu as pltpu
from jax.sharding import PartitionSpec as P

CALB = 16384
CPAR = 64
KNOTS = 1024
OBS = 64
SLOTS = 4
AXES = ("grp", "mem")
F32 = jnp.float32
BF16 = jnp.bfloat16
VMEM = pl.BlockSpec(memory_space=pltpu.VMEM)
SMEM = pl.BlockSpec(memory_space=pltpu.SMEM)
HBM = pl.BlockSpec(memory_space=pltpu.HBM)
LIMIT = pltpu.CompilerParams(vmem_limit_bytes=24 * 1024 * 1024)


def far(array):
    return pltpu.with_memory_space_constraint(array, pltpu.HBM)
NT = (((1,), (1,)), ((), ()))
TN = (((0,), (0,)), ((), ()))


def halves(value):
    top = value.astype(BF16)
    return top, (value - top.astype(F32)).astype(BF16)


def slots_of(row):
    slots = row.shape[1]
    owner = row >> 6
    column = jnp.broadcast_to(owner.astype(F32), (128, slots)).T[:, 0:1]
    before = lax.broadcasted_iota(jnp.int32, (slots, slots), 0) < lax.broadcasted_iota(jnp.int32, (slots, slots), 1)
    same = (column == owner.astype(F32)) & before
    rank = jnp.sum(same.astype(F32), axis=0, keepdims=True)
    offset = (row & 63).astype(F32)
    owners = [jnp.where(rank == float(j), owner.astype(F32), -1.0) for j in range(SLOTS)]
    return jnp.concatenate(owners + [jnp.where(rank == float(j), offset, 0.0) for j in range(SLOTS)], axis=0)


def source_kernel(
    count_ref, obs_hbm, wt_hbm, js_hbm, ap_hbm, seg_hbm,
    sums_ref, upd_ref, resid_ref,
    obs_ref, wt_ref, js_ref, ap_ref, seg_ref, terms, sems,
):
    pairs = ((obs_hbm, obs_ref), (wt_hbm, wt_ref), (js_hbm, js_ref), (ap_hbm, ap_ref), (seg_hbm, seg_ref))
    copies = [pltpu.make_async_copy(src, dst, sems.at[i]) for i, (src, dst) in enumerate(pairs)]
    for copy in copies:
        copy.start()
    for copy in copies[0:3]:
        copy.wait()
    rows, slots = obs_ref.shape
    lane = lax.broadcasted_iota(jnp.int32, (1, slots), 1)
    used = (lane < count_ref[0]).astype(F32)
    live = wt_ref[...] * used
    obs = obs_ref[...]
    weighted = live * obs
    resid = obs
    for k in range(5):
        jac = js_ref[k]
        numer = jnp.sum(jac * weighted, axis=0, keepdims=True)
        denom = 1.0 + jnp.sum(jac * jac * live, axis=0, keepdims=True)
        update = numer / denom
        upd_ref[k : k + 1, :] = update
        resid = resid - jac * update
    resid_ref[...] = resid
    copies[3].wait()
    copies[4].wait()
    live_resid = live * resid
    for k in range(4):
        part = ap_ref[k]
        grad = part * live_resid
        diag = part * part * live
        for c in range(slots // 128):
            terms[c, pl.ds(k, rows, stride=8), :] = grad[:, 128 * c : 128 * c + 128]
            terms[c, pl.ds(4 + k, rows, stride=8), :] = diag[:, 128 * c : 128 * c + 128]
    ids = lax.broadcasted_iota(jnp.int32, (16, slots), 0).astype(F32).astype(BF16)
    batch = 4

    def step(i, total):
        left, right = [], []
        for b in range(batch):
            r = i * batch + b
            seg = seg_ref[pl.ds(r, 1), :]
            high = jnp.broadcast_to((seg >> 7).astype(F32), (16, slots)).astype(BF16)
            low = jnp.broadcast_to((seg & 127).astype(F32), (16, slots)).astype(BF16)
            place = pl.ds(pl.multiple_of(r * 8, 8), 8)
            value = jnp.concatenate([terms[c, place, :] for c in range(slots // 128)], axis=1)
            top = value.astype(BF16).astype(F32)
            both = jnp.concatenate([value, value - top], axis=0).astype(BF16)
            zero = jnp.zeros_like(both)
            one = jnp.ones_like(both)
            left.append(jnp.concatenate([jnp.where(high == jnp.asarray(h, BF16), both, zero) for h in range(8)], axis=0))
            right.append(jnp.concatenate([jnp.where(low == ids + jnp.asarray(16 * g, BF16), one, zero) for g in range(8)], axis=0))
        return total + lax.dot_general(
            jnp.concatenate(left, axis=1), jnp.concatenate(right, axis=1), NT, preferred_element_type=F32
        )

    total = lax.fori_loop(0, rows // batch, step, jnp.zeros((128, 128), F32))
    for h in range(8):
        sums_ref[8 * h : 8 * h + 8, :] = total[16 * h : 16 * h + 8] + total[16 * h + 8 : 16 * h + 16]


def pick_rows(code_ref, j, owners):
    slots = code_ref.shape[1]
    ids = lax.broadcasted_iota(jnp.int32, (owners, slots), 0).astype(F32).astype(BF16)
    code = jnp.broadcast_to(code_ref[j : j + 1, :], (owners, slots)).astype(BF16)
    return jnp.where(ids == code, jnp.ones_like(code), jnp.zeros_like(code))


def near_kernel(count_ref, cal_ref, wt_hbm, ap_hbm, seg_hbm, jac_hbm, live_ref, ap_ref, seg_ref, jac_ref, code_ref, sems):
    pairs = ((wt_hbm, live_ref), (ap_hbm, ap_ref), (seg_hbm, seg_ref), (jac_hbm, jac_ref))
    copies = [pltpu.make_async_copy(src, dst, sems.at[i]) for i, (src, dst) in enumerate(pairs)]
    for copy in copies:
        copy.start()
    code_ref[...] = slots_of(cal_ref[...])
    copies[0].wait()
    lane = lax.broadcasted_iota(jnp.int32, (1, live_ref.shape[1]), 1)
    live_ref[...] = live_ref[...] * (lane < count_ref[0]).astype(F32)
    for copy in copies[1:]:
        copy.wait()


def early_kernel(live_ref, jac_ref, code_ref, send_ref, terms):
    rows, slots = live_ref.shape
    for c in range(slots // 128):
        lanes = slice(128 * c, 128 * c + 128)

        def blocks(i, diag):
            live = live_ref[pl.ds(pl.multiple_of(i * 8, 8), 8), lanes]
            for b in range(8):
                jac = jac_ref[i * 8 + b, :, lanes].astype(F32)
                diag = diag + jac * jac * live[b : b + 1]
            return diag

        terms[:, lanes] = lax.fori_loop(0, rows // 8, blocks, jnp.zeros((CPAR, 128), F32))
    top, rest = halves(terms[...])
    blank = jnp.zeros_like(top)
    both = jnp.concatenate([blank, top, blank, rest], axis=0)
    owners = send_ref.shape[0] // (SLOTS + 1)
    anywhere = jnp.zeros((owners, slots), BF16)
    for j in range(SLOTS):
        pick = pick_rows(code_ref, j, owners)
        anywhere = anywhere + pick
        moved = lax.dot_general(pick, both, NT, preferred_element_type=F32)
        send_ref[pl.ds(j, owners, stride=SLOTS + 1), :] = moved[:, 0:128] + moved[:, 128:256]
    offsets = jnp.concatenate([code_ref[SLOTS : 2 * SLOTS, :], jnp.zeros((128 - SLOTS, slots), F32)], axis=0).astype(BF16)
    moved = lax.dot_general(anywhere, offsets, NT, preferred_element_type=F32)
    send_ref[pl.ds(SLOTS, owners, stride=SLOTS + 1), :] = moved


def residual_kernel(
    place_ref, sums_ref, live_ref, ap_ref, seg_ref, jac_ref, resid_ref, code_ref, early_ref, att_ref, out_ref, send_ref, vec_buf, terms
):
    rows, slots = live_ref.shape
    tables = []
    for h in range(8):
        tile = sums_ref[8 * h : 8 * h + 8, :]
        tables.append(tile[0:4] / (1.0 + tile[4:8]))
    tile = sums_ref[pl.ds(pl.multiple_of((place_ref[0] // 2) * 8, 8), 8), :]
    mine = tile[0:4] / (1.0 + tile[4:8])
    att_ref[...] = jnp.where(lax.rem(place_ref[0], 2) == 0, mine[:, 0:64], mine[:, 64:128])

    def look(i, carry):
        base = pl.multiple_of(i * 8, 8)
        for c in range(slots // 128):
            lanes = slice(128 * c, 128 * c + 128)
            seg = seg_ref[pl.ds(base, 8), lanes]
            low = seg & 127
            high = seg >> 7
            new = resid_ref[pl.ds(base, 8), lanes]
            masks = [high == h for h in range(8)]
            for k in range(4):
                found = jnp.zeros((8, 128), F32)
                for h in range(8):
                    table = jnp.broadcast_to(tables[h][k : k + 1, :], (8, 128))
                    found = jnp.where(masks[h], jnp.take_along_axis(table, low, axis=1), found)
                new = new - ap_ref[k, pl.ds(base, 8), lanes] * found
            out_ref[pl.ds(base, 8), lanes] = new
            vec_buf[pl.ds(base, 8), lanes] = new * live_ref[pl.ds(base, 8), lanes]
        return carry

    lax.fori_loop(0, rows // 8, look, 0)
    for c in range(slots // 128):
        lanes = slice(128 * c, 128 * c + 128)

        def blocks(i, grad):
            vec = vec_buf[pl.ds(pl.multiple_of(i * 8, 8), 8), lanes]
            for b in range(8):
                grad = grad + jac_ref[i * 8 + b, :, lanes].astype(F32) * vec[b : b + 1]
            return grad

        terms[:, lanes] = lax.fori_loop(0, rows // 8, blocks, jnp.zeros((CPAR, 128), F32))
    top, rest = halves(terms[...])
    blank = jnp.zeros_like(top)
    both = jnp.concatenate([top, blank, rest, blank], axis=0)
    owners = send_ref.shape[0] // (SLOTS + 1)
    for j in range(SLOTS):
        moved = lax.dot_general(pick_rows(code_ref, j, owners), both, NT, preferred_element_type=F32)
        part = pl.ds(j, owners, stride=SLOTS + 1)
        send_ref[part, :] = early_ref[part, :] + moved[:, 0:128] + moved[:, 128:256]
    part = pl.ds(SLOTS, owners, stride=SLOTS + 1)
    send_ref[part, :] = early_ref[part, :]


def gather_kernel(got_ref, out_ref):
    devices = got_ref.shape[0] // (SLOTS + 1)
    ids = lax.broadcasted_iota(jnp.int32, (devices, 64), 1).astype(F32)
    offsets = got_ref[pl.ds(SLOTS, devices, stride=SLOTS + 1), :]
    total = jnp.zeros((64, 256), F32)
    for j in range(SLOTS):
        pick = (ids == offsets[:, j : j + 1]).astype(F32).astype(BF16)
        top, rest = halves(got_ref[pl.ds(j, devices, stride=SLOTS + 1), :])
        total = total + lax.dot_general(pick, jnp.concatenate([top, rest], axis=1), TN, preferred_element_type=F32)
    sums = total[:, 0:128] + total[:, 128:256]
    out_ref[...] = sums[:, 0:CPAR] / (1.0 + sums[:, CPAR : 2 * CPAR])


def step_pairs(core, x, y, z):
    pairs = []
    for i in range(256):
        grp, mem = divmod(i, 16)
        c, px, py, pz = mem & 1, (mem >> 1) & 3, ((mem >> 3) << 1) | (grp >> 3), grp & 7
        c, px, py, pz = c ^ core, px ^ x, py ^ y, pz ^ z
        pairs.append((i, ((py & 1) * 8 + pz) * 16 + (py >> 1) * 8 + px * 2 + c))
    return pairs


def moved(value, *step):
    return lax.ppermute(value, AXES, step_pairs(*step))


def body(obs_resid, weight, jac_src, att_part, seg_index, jac_cal, cal_index, block_count):
    slots = obs_resid.shape[0]
    devices = lax.axis_size(AXES)
    obs, wt, seg = far(obs_resid.T), far(weight.T), far(seg_index.T)
    js, ap = far(jac_src.transpose(0, 2, 1)), far(att_part.transpose(0, 2, 1))
    jac = far(jac_cal.transpose(1, 2, 0))
    plane = pltpu.VMEM((OBS, slots), F32)
    rows = pltpu.VMEM((devices * (SLOTS + 1), 128), F32)
    sums, src_update, resid_one = pl.pallas_call(
        source_kernel,
        out_shape=(pltpu.VMEM((64, 128), F32), jax.ShapeDtypeStruct((5, slots), F32), plane),
        in_specs=[SMEM] + [HBM] * 5,
        out_specs=(VMEM,) * 3,
        scratch_shapes=[
            pltpu.VMEM((OBS, slots), F32),
            pltpu.VMEM((OBS, slots), F32),
            pltpu.VMEM((5, OBS, slots), F32),
            pltpu.VMEM((4, OBS, slots), F32),
            pltpu.VMEM((OBS, slots), jnp.int32),
            pltpu.VMEM((slots // 128, OBS * 8, 128), F32),
            pltpu.SemaphoreType.DMA((5,)),
        ],
        compiler_params=LIMIT,
        name="source_step",
    )(block_count, obs, wt, js, ap, seg)
    live, near_ap, near_seg, near_jac, code = pl.pallas_call(
        near_kernel,
        out_shape=(
            plane,
            pltpu.VMEM((4, OBS, slots), F32),
            pltpu.VMEM((OBS, slots), jnp.int32),
            pltpu.VMEM((OBS, CPAR, slots), BF16),
            pltpu.VMEM((2 * SLOTS, slots), F32),
        ),
        in_specs=[SMEM, VMEM] + [HBM] * 4,
        out_specs=(VMEM,) * 5,
        scratch_shapes=[pltpu.SemaphoreType.DMA((4,))],
        compiler_params=LIMIT,
        name="near_step",
    )(block_count, cal_index[None, :], wt, ap, seg, jac)
    early = pl.pallas_call(
        early_kernel,
        out_shape=rows,
        in_specs=[VMEM] * 3,
        out_specs=VMEM,
        scratch_shapes=[pltpu.VMEM((CPAR, slots), F32)],
        compiler_params=LIMIT,
        name="early_step",
    )(live, near_jac, code)
    total = sums + moved(sums, 1, 0, 0, 0)
    total = (total + moved(total, 0, 1, 0, 0)) + (moved(total, 0, 2, 0, 0) + moved(total, 0, 3, 0, 0))
    total = (total + moved(total, 0, 0, 1, 0)) + (moved(total, 0, 0, 2, 0) + moved(total, 0, 0, 3, 0))
    total = total + moved(total, 0, 0, 0, 1)
    total = total + moved(total, 0, 0, 0, 2)
    total = total + moved(total, 0, 0, 0, 6)
    place = lax.axis_index("mem").astype(jnp.int32)[None]
    att_out, new_resid, send = pl.pallas_call(
        residual_kernel,
        out_shape=(
            jax.ShapeDtypeStruct((4, KNOTS // lax.axis_size("mem")), F32),
            jax.ShapeDtypeStruct((OBS, slots), F32),
            rows,
        ),
        in_specs=[SMEM] + [VMEM] * 8,
        out_specs=(VMEM,) * 3,
        scratch_shapes=[pltpu.VMEM((OBS, slots), F32), pltpu.VMEM((CPAR, slots), F32)],
        compiler_params=LIMIT,
        name="residual_step",
    )(place, total, live, near_ap, near_seg, near_jac, resid_one, code, early)
    got = lax.all_to_all(send.reshape(devices, 1, -1), AXES, 0, 0, tiled=True)
    cal_update = pl.pallas_call(
        gather_kernel,
        out_shape=jax.ShapeDtypeStruct((CALB // devices, CPAR), F32),
        in_specs=[VMEM],
        out_specs=VMEM,
        compiler_params=LIMIT,
        name="calibration_step",
    )(got.reshape(rows.shape))
    return src_update, att_out, cal_update, new_resid.T


def solution(mesh):
    return jax.shard_map(
        body,
        mesh=mesh,
        in_specs=(
            P(AXES, None),
            P(AXES, None),
            P(None, AXES, None),
            P(None, AXES, None),
            P(AXES, None),
            P(AXES, None, None),
            P(AXES),
            P(AXES),
        ),
        out_specs=(P(None, AXES), P(None, "mem"), P(AXES, None), P(AXES, None)),
        check_vma=False,
    )
```

```python
import jax
import jax.numpy as jnp
from jax import lax
from jax.experimental import pallas as pl
from jax.experimental.pallas import tpu as pltpu
from jax.sharding import PartitionSpec as P

CALB = 16384
CPAR = 64
KNOTS = 1024
OBS = 64
SLOTS = 4
AXES = ("grp", "mem")
F32 = jnp.float32
BF16 = jnp.bfloat16
VMEM = pl.BlockSpec(memory_space=pltpu.VMEM)
SMEM = pl.BlockSpec(memory_space=pltpu.SMEM)
HBM = pl.BlockSpec(memory_space=pltpu.HBM)
LIMIT = pltpu.CompilerParams(vmem_limit_bytes=24 * 1024 * 1024)


def far(array):
    return pltpu.with_memory_space_constraint(array, pltpu.HBM)
NT = (((1,), (1,)), ((), ()))
TN = (((0,), (0,)), ((), ()))


def halves(value):
    top = value.astype(BF16)
    return top, (value - top.astype(F32)).astype(BF16)


def slots_of(row):
    slots = row.shape[1]
    owner = row >> 6
    column = jnp.broadcast_to(owner.astype(F32), (128, slots)).T[:, 0:1]
    before = lax.broadcasted_iota(jnp.int32, (slots, slots), 0) < lax.broadcasted_iota(jnp.int32, (slots, slots), 1)
    same = (column == owner.astype(F32)) & before
    rank = jnp.sum(same.astype(F32), axis=0, keepdims=True)
    offset = (row & 63).astype(F32)
    owners = [jnp.where(rank == float(j), owner.astype(F32), -1.0) for j in range(SLOTS)]
    return jnp.concatenate(owners + [jnp.where(rank == float(j), offset, 0.0) for j in range(SLOTS)], axis=0)


def source_kernel(
    count_ref, obs_hbm, wt_hbm, js_hbm, ap_hbm, seg_hbm,
    sums_ref, upd_ref, resid_ref,
    obs_ref, wt_ref, js_ref, ap_ref, seg_ref, terms, sems,
):
    pairs = ((obs_hbm, obs_ref), (wt_hbm, wt_ref), (js_hbm, js_ref), (ap_hbm, ap_ref), (seg_hbm, seg_ref))
    copies = [pltpu.make_async_copy(src, dst, sems.at[i]) for i, (src, dst) in enumerate(pairs)]
    for copy in copies:
        copy.start()
    for copy in copies[0:3]:
        copy.wait()
    rows, slots = obs_ref.shape
    lane = lax.broadcasted_iota(jnp.int32, (1, slots), 1)
    used = (lane < count_ref[0]).astype(F32)
    live = wt_ref[...] * used
    obs = obs_ref[...]
    weighted = live * obs
    resid = obs
    for k in range(5):
        jac = js_ref[k]
        numer = jnp.sum(jac * weighted, axis=0, keepdims=True)
        denom = 1.0 + jnp.sum(jac * jac * live, axis=0, keepdims=True)
        update = numer / denom
        upd_ref[k : k + 1, :] = update
        resid = resid - jac * update
    resid_ref[...] = resid
    copies[3].wait()
    copies[4].wait()
    live_resid = live * resid
    for k in range(4):
        part = ap_ref[k]
        grad = part * live_resid
        diag = part * part * live
        for c in range(slots // 128):
            terms[c, pl.ds(k, rows, stride=8), :] = grad[:, 128 * c : 128 * c + 128]
            terms[c, pl.ds(4 + k, rows, stride=8), :] = diag[:, 128 * c : 128 * c + 128]
    ids = lax.broadcasted_iota(jnp.int32, (16, slots), 0).astype(F32).astype(BF16)
    left, right = [], []
    for r in range(rows):
        seg = seg_ref[r : r + 1, :]
        high = jnp.broadcast_to((seg >> 7).astype(F32), (16, slots)).astype(BF16)
        low = jnp.broadcast_to((seg & 127).astype(F32), (16, slots)).astype(BF16)
        value = jnp.concatenate([terms[c, 8 * r : 8 * r + 8, :] for c in range(slots // 128)], axis=1)
        top = value.astype(BF16).astype(F32)
        both = jnp.concatenate([value, value - top], axis=0).astype(BF16)
        zero = jnp.zeros_like(both)
        one = jnp.ones_like(both)
        left.append(jnp.concatenate([jnp.where(high == jnp.asarray(h, BF16), both, zero) for h in range(8)], axis=0))
        right.append(jnp.concatenate([jnp.where(low == ids + jnp.asarray(16 * g, BF16), one, zero) for g in range(8)], axis=0))
    total = lax.dot_general(jnp.concatenate(left, axis=1), jnp.concatenate(right, axis=1), NT, preferred_element_type=F32)
    for h in range(8):
        sums_ref[8 * h : 8 * h + 8, :] = total[16 * h : 16 * h + 8] + total[16 * h + 8 : 16 * h + 16]


def pick_rows(code_ref, j, owners):
    slots = code_ref.shape[1]
    ids = lax.broadcasted_iota(jnp.int32, (owners, slots), 0).astype(F32).astype(BF16)
    code = jnp.broadcast_to(code_ref[j : j + 1, :], (owners, slots)).astype(BF16)
    return jnp.where(ids == code, jnp.ones_like(code), jnp.zeros_like(code))


def near_kernel(
    count_ref, cal_hbm, wt_hbm, ap_hbm, seg_hbm, jac_hbm, live_ref, ap_ref, seg_ref, jac_ref, code_ref, send_ref, cal_ref, terms, sems
):
    rows, slots = live_ref.shape
    step = rows // 4
    pairs = [(cal_hbm, cal_ref), (wt_hbm, live_ref)]
    pairs += [(jac_hbm.at[pl.ds(step * q, step)], jac_ref.at[pl.ds(step * q, step)]) for q in range(4)]
    pairs += [(ap_hbm, ap_ref), (seg_hbm, seg_ref)]
    copies = [pltpu.make_async_copy(src, dst, sems.at[i]) for i, (src, dst) in enumerate(pairs)]
    for copy in copies:
        copy.start()
    copies[0].wait()
    code_ref[...] = slots_of(cal_ref[...])
    copies[1].wait()
    lane = lax.broadcasted_iota(jnp.int32, (1, slots), 1)
    live_ref[...] = live_ref[...] * (lane < count_ref[0]).astype(F32)
    for q in range(4):
        copies[2 + q].wait()
        for c in range(slots // 128):
            lanes = slice(128 * c, 128 * c + 128)
            diag = jnp.zeros((CPAR, 128), F32) if q == 0 else terms[:, lanes]
            for r in range(step * q, step * q + step):
                jac = jac_ref[r, :, lanes].astype(F32)
                diag = diag + jac * jac * live_ref[r : r + 1, lanes]
            terms[:, lanes] = diag
    top, rest = halves(terms[...])
    blank = jnp.zeros_like(top)
    both = jnp.concatenate([blank, top, blank, rest], axis=0)
    owners = send_ref.shape[0] // (SLOTS + 1)
    anywhere = jnp.zeros((owners, slots), BF16)
    for j in range(SLOTS):
        pick = pick_rows(code_ref, j, owners)
        anywhere = anywhere + pick
        moved = lax.dot_general(pick, both, NT, preferred_element_type=F32)
        send_ref[pl.ds(j, owners, stride=SLOTS + 1), :] = moved[:, 0:128] + moved[:, 128:256]
    offsets = jnp.concatenate([code_ref[SLOTS : 2 * SLOTS, :], jnp.zeros((128 - SLOTS, slots), F32)], axis=0).astype(BF16)
    moved = lax.dot_general(anywhere, offsets, NT, preferred_element_type=F32)
    send_ref[pl.ds(SLOTS, owners, stride=SLOTS + 1), :] = moved
    for copy in copies[6:]:
        copy.wait()


def residual_kernel(
    sums_ref, live_ref, ap_ref, seg_ref, jac_ref, resid_ref, code_ref, early_ref, att_ref, out_ref, send_ref, vec_buf, terms
):
    rows, slots = live_ref.shape
    tables = []
    for h in range(8):
        tile = sums_ref[8 * h : 8 * h + 8, :]
        tables.append(tile[0:4] / (1.0 + tile[4:8]))
    place = lax.axis_index("mem")
    tile = sums_ref[pl.ds(pl.multiple_of((place // 2) * 8, 8), 8), :]
    mine = tile[0:4] / (1.0 + tile[4:8])
    att_ref[...] = jnp.where(lax.rem(place, 2) == 0, mine[:, 0:64], mine[:, 64:128])

    for i in range(rows // 8):
        block = slice(8 * i, 8 * i + 8)
        for c in range(slots // 128):
            lanes = slice(128 * c, 128 * c + 128)
            seg = seg_ref[block, lanes]
            low = seg & 127
            bits = [(seg & (128 << n)) != 0 for n in range(3)]
            new = resid_ref[block, lanes]
            for k in range(4):
                found = [jnp.take_along_axis(jnp.broadcast_to(table[k : k + 1, :], (8, 128)), low, axis=1) for table in tables]
                for bit in bits:
                    found = [jnp.where(bit, odd, even) for even, odd in zip(found[0::2], found[1::2])]
                new = new - ap_ref[k, block, lanes] * found[0]
            out_ref[block, lanes] = new
            vec_buf[block, lanes] = new * live_ref[block, lanes]
    for c in range(slots // 128):
        lanes = slice(128 * c, 128 * c + 128)

        def blocks(i, grad):
            vec = vec_buf[pl.ds(pl.multiple_of(i * 8, 8), 8), lanes]
            for b in range(8):
                grad = grad + jac_ref[i * 8 + b, :, lanes].astype(F32) * vec[b : b + 1]
            return grad

        terms[:, lanes] = lax.fori_loop(0, rows // 8, blocks, jnp.zeros((CPAR, 128), F32), unroll=4)
    top, rest = halves(terms[...])
    blank = jnp.zeros_like(top)
    both = jnp.concatenate([top, blank, rest, blank], axis=0)
    owners = send_ref.shape[0] // (SLOTS + 1)
    for j in range(SLOTS):
        moved = lax.dot_general(pick_rows(code_ref, j, owners), both, NT, preferred_element_type=F32)
        part = pl.ds(j, owners, stride=SLOTS + 1)
        send_ref[part, :] = early_ref[part, :] + moved[:, 0:128] + moved[:, 128:256]
    part = pl.ds(SLOTS, owners, stride=SLOTS + 1)
    send_ref[part, :] = early_ref[part, :]


def gather_kernel(got_ref, out_ref):
    devices = got_ref.shape[0] // (SLOTS + 1)
    ids = lax.broadcasted_iota(jnp.int32, (devices, 64), 1).astype(F32)
    offsets = got_ref[pl.ds(SLOTS, devices, stride=SLOTS + 1), :]
    total = jnp.zeros((64, 256), F32)
    for j in range(SLOTS):
        pick = (ids == offsets[:, j : j + 1]).astype(F32).astype(BF16)
        top, rest = halves(got_ref[pl.ds(j, devices, stride=SLOTS + 1), :])
        total = total + lax.dot_general(pick, jnp.concatenate([top, rest], axis=1), TN, preferred_element_type=F32)
    sums = total[:, 0:128] + total[:, 128:256]
    out_ref[...] = sums[:, 0:CPAR] / (1.0 + sums[:, CPAR : 2 * CPAR])


def step_pairs(core, x, y, z):
    pairs = []
    for i in range(256):
        grp, mem = divmod(i, 16)
        c, px, py, pz = mem & 1, (mem >> 1) & 3, ((mem >> 3) << 1) | (grp >> 3), grp & 7
        c, px, py, pz = c ^ core, px ^ x, py ^ y, pz ^ z
        pairs.append((i, ((py & 1) * 8 + pz) * 16 + (py >> 1) * 8 + px * 2 + c))
    return pairs


def moved(value, *step):
    return lax.ppermute(value, AXES, step_pairs(*step))


def body(obs_resid, weight, jac_src, att_part, seg_index, jac_cal, cal_index, block_count):
    slots = obs_resid.shape[0]
    devices = lax.axis_size(AXES)
    obs, wt, seg = far(obs_resid.T), far(weight.T), far(seg_index.T)
    js, ap = far(jac_src.transpose(0, 2, 1)), far(att_part.transpose(0, 2, 1))
    jac = far(jac_cal.transpose(1, 2, 0))
    plane = pltpu.VMEM((OBS, slots), F32)
    rows = pltpu.VMEM((devices * (SLOTS + 1), 128), F32)
    sums, src_update, resid_one = pl.pallas_call(
        source_kernel,
        out_shape=(pltpu.VMEM((64, 128), F32), jax.ShapeDtypeStruct((5, slots), F32), plane),
        in_specs=[SMEM] + [HBM] * 5,
        out_specs=(VMEM,) * 3,
        scratch_shapes=[
            pltpu.VMEM((OBS, slots), F32),
            pltpu.VMEM((OBS, slots), F32),
            pltpu.VMEM((5, OBS, slots), F32),
            pltpu.VMEM((4, OBS, slots), F32),
            pltpu.VMEM((OBS, slots), jnp.int32),
            pltpu.VMEM((slots // 128, OBS * 8, 128), F32),
            pltpu.SemaphoreType.DMA((5,)),
        ],
        compiler_params=LIMIT,
        name="source_step",
    )(block_count, obs, wt, js, ap, seg)
    live, near_ap, near_seg, near_jac, code, early = pl.pallas_call(
        near_kernel,
        out_shape=(
            plane,
            pltpu.VMEM((4, OBS, slots), F32),
            pltpu.VMEM((OBS, slots), jnp.int32),
            pltpu.VMEM((OBS, CPAR, slots), BF16),
            pltpu.VMEM((2 * SLOTS, slots), F32),
            rows,
        ),
        in_specs=[SMEM] + [HBM] * 5,
        out_specs=(VMEM,) * 6,
        scratch_shapes=[pltpu.VMEM((1, slots), jnp.int32), pltpu.VMEM((CPAR, slots), F32), pltpu.SemaphoreType.DMA((8,))],
        compiler_params=LIMIT,
        name="near_step",
    )(block_count, far(cal_index[None, :]), wt, ap, seg, jac)
    total = sums + moved(sums, 1, 0, 0, 0)
    total = (total + moved(total, 0, 1, 0, 0)) + (moved(total, 0, 2, 0, 0) + moved(total, 0, 3, 0, 0))
    total = (total + moved(total, 0, 0, 1, 0)) + (moved(total, 0, 0, 2, 0) + moved(total, 0, 0, 3, 0))
    total = total + moved(total, 0, 0, 0, 1)
    total, code = lax.optimization_barrier((total, code))
    total = total + moved(total, 0, 0, 0, 2)
    total = total + moved(total, 0, 0, 0, 6)
    att_out, new_resid, send = pl.pallas_call(
        residual_kernel,
        out_shape=(
            jax.ShapeDtypeStruct((4, KNOTS // lax.axis_size("mem")), F32),
            jax.ShapeDtypeStruct((OBS, slots), F32),
            rows,
        ),
        in_specs=[VMEM] * 8,
        out_specs=(VMEM,) * 3,
        scratch_shapes=[pltpu.VMEM((OBS, slots), F32), pltpu.VMEM((CPAR, slots), F32)],
        compiler_params=LIMIT,
        name="residual_step",
    )(total, live, near_ap, near_seg, near_jac, resid_one, code, early)
    got = lax.all_to_all(send.reshape(devices, 1, -1), AXES, 0, 0, tiled=True)
    cal_update = pl.pallas_call(
        gather_kernel,
        out_shape=jax.ShapeDtypeStruct((CALB // devices, CPAR), F32),
        in_specs=[VMEM],
        out_specs=VMEM,
        compiler_params=LIMIT,
        name="calibration_step",
    )(got.reshape(rows.shape))
    return src_update, att_out, cal_update, new_resid.T


def solution(mesh):
    return jax.shard_map(
        body,
        mesh=mesh,
        in_specs=(
            P(AXES, None),
            P(AXES, None),
            P(None, AXES, None),
            P(None, AXES, None),
            P(AXES, None),
            P(AXES, None, None),
            P(AXES),
            P(AXES),
        ),
        out_specs=(P(None, AXES), P(None, "mem"), P(AXES, None), P(AXES, None)),
        check_vma=False,
    )
```

```python
import jax
import jax.numpy as jnp
from jax import lax
from jax.experimental import pallas as pl
from jax.experimental.pallas import tpu as pltpu
from jax.sharding import PartitionSpec as P

CALB = 16384
CPAR = 64
KNOTS = 1024
OBS = 64
SLOTS = 4
AXES = ("grp", "mem")
F32 = jnp.float32
BF16 = jnp.bfloat16
VMEM = pl.BlockSpec(memory_space=pltpu.VMEM)
SMEM = pl.BlockSpec(memory_space=pltpu.SMEM)
HBM = pl.BlockSpec(memory_space=pltpu.HBM)
LIMIT = pltpu.CompilerParams(vmem_limit_bytes=24 * 1024 * 1024)


def far(array):
    return pltpu.with_memory_space_constraint(array, pltpu.HBM)
NT = (((1,), (1,)), ((), ()))
TN = (((0,), (0,)), ((), ()))


def halves(value):
    top = value.astype(BF16)
    return top, (value - top.astype(F32)).astype(BF16)


def slots_of(row):
    slots = row.shape[1]
    owner = row >> 6
    column = jnp.broadcast_to(owner.astype(F32), (128, slots)).T[:, 0:1]
    before = lax.broadcasted_iota(jnp.int32, (slots, slots), 0) < lax.broadcasted_iota(jnp.int32, (slots, slots), 1)
    same = (column == owner.astype(F32)) & before
    rank = jnp.sum(same.astype(F32), axis=0, keepdims=True)
    offset = (row & 63).astype(F32)
    owners = [jnp.where(rank == float(j), owner.astype(F32), -1.0) for j in range(SLOTS)]
    return jnp.concatenate(owners + [jnp.where(rank == float(j), offset, 0.0) for j in range(SLOTS)], axis=0)


def source_kernel(
    count_ref, obs_hbm, wt_hbm, js_hbm, ap_hbm, seg_hbm,
    sums_ref, upd_ref, resid_ref,
    obs_ref, wt_ref, js_ref, ap_ref, seg_ref, terms, sems,
):
    pairs = ((obs_hbm, obs_ref), (wt_hbm, wt_ref), (js_hbm, js_ref), (ap_hbm, ap_ref), (seg_hbm, seg_ref))
    copies = [pltpu.make_async_copy(src, dst, sems.at[i]) for i, (src, dst) in enumerate(pairs)]
    for copy in copies:
        copy.start()
    for copy in copies[0:3]:
        copy.wait()
    rows, slots = obs_ref.shape
    lane = lax.broadcasted_iota(jnp.int32, (1, slots), 1)
    used = (lane < count_ref[0]).astype(F32)
    live = wt_ref[...] * used
    obs = obs_ref[...]
    weighted = live * obs
    resid = obs
    for k in range(5):
        jac = js_ref[k]
        numer = jnp.sum(jac * weighted, axis=0, keepdims=True)
        denom = 1.0 + jnp.sum(jac * jac * live, axis=0, keepdims=True)
        update = numer / denom
        upd_ref[k : k + 1, :] = update
        resid = resid - jac * update
    resid_ref[...] = resid
    copies[3].wait()
    copies[4].wait()
    live_resid = live * resid
    for k in range(4):
        part = ap_ref[k]
        grad = part * live_resid
        diag = part * part * live
        for c in range(slots // 128):
            terms[c, pl.ds(k, rows, stride=8), :] = grad[:, 128 * c : 128 * c + 128]
            terms[c, pl.ds(4 + k, rows, stride=8), :] = diag[:, 128 * c : 128 * c + 128]
    ids = lax.broadcasted_iota(jnp.int32, (16, slots), 0).astype(F32).astype(BF16)
    left, right = [], []
    for r in range(rows):
        seg = seg_ref[r : r + 1, :]
        high = jnp.broadcast_to((seg >> 7).astype(F32), (16, slots)).astype(BF16)
        low = jnp.broadcast_to((seg & 127).astype(F32), (16, slots)).astype(BF16)
        value = jnp.concatenate([terms[c, 8 * r : 8 * r + 8, :] for c in range(slots // 128)], axis=1)
        top = value.astype(BF16).astype(F32)
        both = jnp.concatenate([value, value - top], axis=0).astype(BF16)
        zero = jnp.zeros_like(both)
        one = jnp.ones_like(both)
        left.append(jnp.concatenate([jnp.where(high == jnp.asarray(h, BF16), both, zero) for h in range(8)], axis=0))
        right.append(jnp.concatenate([jnp.where(low == ids + jnp.asarray(16 * g, BF16), one, zero) for g in range(8)], axis=0))
    total = lax.dot_general(jnp.concatenate(left, axis=1), jnp.concatenate(right, axis=1), NT, preferred_element_type=F32)
    for h in range(8):
        sums_ref[8 * h : 8 * h + 8, :] = total[16 * h : 16 * h + 8] + total[16 * h + 8 : 16 * h + 16]


def pick_rows(code_ref, j, owners):
    slots = code_ref.shape[1]
    ids = lax.broadcasted_iota(jnp.int32, (owners, slots), 0).astype(F32).astype(BF16)
    code = jnp.broadcast_to(code_ref[j : j + 1, :], (owners, slots)).astype(BF16)
    return jnp.where(ids == code, jnp.ones_like(code), jnp.zeros_like(code))


def near_kernel(
    count_ref, cal_hbm, wt_hbm, ap_hbm, seg_hbm, jac_hbm, live_ref, ap_ref, seg_ref, jac_ref, code_ref, send_ref, cal_ref, terms, sems
):
    rows, slots = live_ref.shape
    step = rows // 4
    pairs = [(cal_hbm, cal_ref), (wt_hbm, live_ref)]
    pairs += [(jac_hbm.at[pl.ds(step * q, step)], jac_ref.at[pl.ds(step * q, step)]) for q in range(4)]
    pairs += [(ap_hbm, ap_ref), (seg_hbm, seg_ref)]
    copies = [pltpu.make_async_copy(src, dst, sems.at[i]) for i, (src, dst) in enumerate(pairs)]
    for copy in copies:
        copy.start()
    copies[0].wait()
    code_ref[...] = slots_of(cal_ref[...])
    copies[1].wait()
    lane = lax.broadcasted_iota(jnp.int32, (1, slots), 1)
    live_ref[...] = live_ref[...] * (lane < count_ref[0]).astype(F32)
    for q in range(4):
        copies[2 + q].wait()
        for c in range(slots // 128):
            lanes = slice(128 * c, 128 * c + 128)
            diag = jnp.zeros((CPAR, 128), F32) if q == 0 else terms[:, lanes]
            for r in range(step * q, step * q + step):
                jac = jac_ref[r, :, lanes].astype(F32)
                diag = diag + jac * jac * live_ref[r : r + 1, lanes]
            terms[:, lanes] = diag
    top, rest = halves(terms[...])
    blank = jnp.zeros_like(top)
    both = jnp.concatenate([blank, top, blank, rest], axis=0)
    owners = send_ref.shape[0] // (SLOTS + 1)
    anywhere = jnp.zeros((owners, slots), BF16)
    for j in range(SLOTS):
        pick = pick_rows(code_ref, j, owners)
        anywhere = anywhere + pick
        moved = lax.dot_general(pick, both, NT, preferred_element_type=F32)
        send_ref[pl.ds(j, owners, stride=SLOTS + 1), :] = moved[:, 0:128] + moved[:, 128:256]
    offsets = jnp.concatenate([code_ref[SLOTS : 2 * SLOTS, :], jnp.zeros((128 - SLOTS, slots), F32)], axis=0).astype(BF16)
    moved = lax.dot_general(anywhere, offsets, NT, preferred_element_type=F32)
    send_ref[pl.ds(SLOTS, owners, stride=SLOTS + 1), :] = moved
    for copy in copies[6:]:
        copy.wait()


def residual_kernel(
    sums_ref, live_ref, ap_ref, seg_ref, jac_ref, resid_ref, code_ref, early_ref, att_ref, out_ref, send_ref, vec_buf, terms
):
    rows, slots = live_ref.shape
    tables = []
    for h in range(8):
        tile = sums_ref[8 * h : 8 * h + 8, :]
        tables.append(tile[0:4] / (1.0 + tile[4:8]))
    place = lax.axis_index("mem")
    tile = sums_ref[pl.ds(pl.multiple_of((place // 2) * 8, 8), 8), :]
    mine = tile[0:4] / (1.0 + tile[4:8])
    att_ref[...] = jnp.where(lax.rem(place, 2) == 0, mine[:, 0:64], mine[:, 64:128])

    for i in range(rows // 8):
        block = slice(8 * i, 8 * i + 8)
        for c in range(slots // 128):
            lanes = slice(128 * c, 128 * c + 128)
            seg = seg_ref[block, lanes]
            low = seg & 127
            bits = [(seg & (128 << n)) != 0 for n in range(3)]
            new = resid_ref[block, lanes]
            for k in range(4):
                found = [jnp.take_along_axis(jnp.broadcast_to(table[k : k + 1, :], (8, 128)), low, axis=1) for table in tables]
                for bit in bits:
                    found = [jnp.where(bit, odd, even) for even, odd in zip(found[0::2], found[1::2])]
                new = new - ap_ref[k, block, lanes] * found[0]
            out_ref[block, lanes] = new
            vec_buf[block, lanes] = new * live_ref[block, lanes]
    for c in range(slots // 128):
        lanes = slice(128 * c, 128 * c + 128)

        def blocks(i, grad):
            vec = vec_buf[pl.ds(pl.multiple_of(i * 8, 8), 8), lanes]
            for b in range(8):
                grad = grad + jac_ref[i * 8 + b, :, lanes].astype(F32) * vec[b : b + 1]
            return grad

        terms[:, lanes] = lax.fori_loop(0, rows // 8, blocks, jnp.zeros((CPAR, 128), F32), unroll=4)
    top, rest = halves(terms[...])
    blank = jnp.zeros_like(top)
    both = jnp.concatenate([top, blank, rest, blank], axis=0)
    owners = send_ref.shape[0] // (SLOTS + 1)
    for j in range(SLOTS):
        moved = lax.dot_general(pick_rows(code_ref, j, owners), both, NT, preferred_element_type=F32)
        part = pl.ds(j, owners, stride=SLOTS + 1)
        send_ref[part, :] = early_ref[part, :] + moved[:, 0:128] + moved[:, 128:256]
    part = pl.ds(SLOTS, owners, stride=SLOTS + 1)
    send_ref[part, :] = early_ref[part, :]


def gather_kernel(got_ref, out_ref):
    devices = got_ref.shape[0] // (SLOTS + 1)
    ids = lax.broadcasted_iota(jnp.int32, (devices, 64), 1).astype(F32)
    offsets = got_ref[pl.ds(SLOTS, devices, stride=SLOTS + 1), :]
    total = jnp.zeros((64, 256), F32)
    for j in range(SLOTS):
        pick = (ids == offsets[:, j : j + 1]).astype(F32).astype(BF16)
        top, rest = halves(got_ref[pl.ds(j, devices, stride=SLOTS + 1), :])
        total = total + lax.dot_general(pick, jnp.concatenate([top, rest], axis=1), TN, preferred_element_type=F32)
    sums = total[:, 0:128] + total[:, 128:256]
    out_ref[...] = sums[:, 0:CPAR] / (1.0 + sums[:, CPAR : 2 * CPAR])


def step_pairs(core, x, y, z):
    pairs = []
    for i in range(256):
        grp, mem = divmod(i, 16)
        c, px, py, pz = mem & 1, (mem >> 1) & 3, ((mem >> 3) << 1) | (grp >> 3), grp & 7
        c, px, py, pz = c ^ core, px ^ x, py ^ y, pz ^ z
        pairs.append((i, ((py & 1) * 8 + pz) * 16 + (py >> 1) * 8 + px * 2 + c))
    return pairs


def moved(value, *step):
    return lax.ppermute(value, AXES, step_pairs(*step))


def body(obs_resid, weight, jac_src, att_part, seg_index, jac_cal, cal_index, block_count):
    slots = obs_resid.shape[0]
    devices = lax.axis_size(AXES)
    obs, wt, seg = far(obs_resid.T), far(weight.T), far(seg_index.T)
    js, ap = far(jac_src.transpose(0, 2, 1)), far(att_part.transpose(0, 2, 1))
    jac = far(jac_cal.transpose(1, 2, 0))
    plane = pltpu.VMEM((OBS, slots), F32)
    rows = pltpu.VMEM((devices * (SLOTS + 1), 128), F32)
    sums, src_update, resid_one = pl.pallas_call(
        source_kernel,
        out_shape=(pltpu.VMEM((64, 128), F32), jax.ShapeDtypeStruct((5, slots), F32), plane),
        in_specs=[SMEM] + [HBM] * 5,
        out_specs=(VMEM,) * 3,
        scratch_shapes=[
            pltpu.VMEM((OBS, slots), F32),
            pltpu.VMEM((OBS, slots), F32),
            pltpu.VMEM((5, OBS, slots), F32),
            pltpu.VMEM((4, OBS, slots), F32),
            pltpu.VMEM((OBS, slots), jnp.int32),
            pltpu.VMEM((slots // 128, OBS * 8, 128), F32),
            pltpu.SemaphoreType.DMA((5,)),
        ],
        compiler_params=LIMIT,
        name="source_step",
    )(block_count, obs, wt, js, ap, seg)
    live, near_ap, near_seg, near_jac, code, early = pl.pallas_call(
        near_kernel,
        out_shape=(
            plane,
            pltpu.VMEM((4, OBS, slots), F32),
            pltpu.VMEM((OBS, slots), jnp.int32),
            pltpu.VMEM((OBS, CPAR, slots), BF16),
            pltpu.VMEM((2 * SLOTS, slots), F32),
            rows,
        ),
        in_specs=[SMEM] + [HBM] * 5,
        out_specs=(VMEM,) * 6,
        scratch_shapes=[pltpu.VMEM((1, slots), jnp.int32), pltpu.VMEM((CPAR, slots), F32), pltpu.SemaphoreType.DMA((8,))],
        compiler_params=LIMIT,
        name="near_step",
    )(block_count, far(cal_index[None, :]), wt, ap, seg, jac)
    total = sums
    total = (total + moved(total, 0, 1, 0, 0)) + (moved(total, 0, 2, 0, 0) + moved(total, 0, 3, 0, 0))
    total = (total + moved(total, 0, 0, 1, 0)) + (moved(total, 0, 0, 2, 0) + moved(total, 0, 0, 3, 0))
    total = (total + moved(total, 0, 0, 0, 1)) + (moved(total, 0, 0, 0, 6) + moved(total, 0, 0, 0, 7))
    total, code = lax.optimization_barrier((total, code))
    total = (total + moved(total, 1, 0, 0, 0)) + (moved(total, 0, 0, 0, 2) + moved(total, 1, 0, 0, 2))
    att_out, new_resid, send = pl.pallas_call(
        residual_kernel,
        out_shape=(
            jax.ShapeDtypeStruct((4, KNOTS // lax.axis_size("mem")), F32),
            jax.ShapeDtypeStruct((OBS, slots), F32),
            rows,
        ),
        in_specs=[VMEM] * 8,
        out_specs=(VMEM,) * 3,
        scratch_shapes=[pltpu.VMEM((OBS, slots), F32), pltpu.VMEM((CPAR, slots), F32)],
        compiler_params=LIMIT,
        name="residual_step",
    )(total, live, near_ap, near_seg, near_jac, resid_one, code, early)
    got = lax.all_to_all(send.reshape(devices, 1, -1), AXES, 0, 0, tiled=True)
    cal_update = pl.pallas_call(
        gather_kernel,
        out_shape=jax.ShapeDtypeStruct((CALB // devices, CPAR), F32),
        in_specs=[VMEM],
        out_specs=VMEM,
        compiler_params=LIMIT,
        name="calibration_step",
    )(got.reshape(rows.shape))
    return src_update, att_out, cal_update, new_resid.T


def solution(mesh):
    return jax.shard_map(
        body,
        mesh=mesh,
        in_specs=(
            P(AXES, None),
            P(AXES, None),
            P(None, AXES, None),
            P(None, AXES, None),
            P(AXES, None),
            P(AXES, None, None),
            P(AXES),
            P(AXES),
        ),
        out_specs=(P(None, AXES), P(None, "mem"), P(AXES, None), P(AXES, None)),
        check_vma=False,
    )
```

```python
import jax
import jax.numpy as jnp
from jax import lax
from jax.experimental import pallas as pl
from jax.experimental.pallas import tpu as pltpu
from jax.sharding import PartitionSpec as P

CALB = 16384
CPAR = 64
KNOTS = 1024
OBS = 64
SLOTS = 4
AXES = ("grp", "mem")
F32 = jnp.float32
BF16 = jnp.bfloat16
VMEM = pl.BlockSpec(memory_space=pltpu.VMEM)
SMEM = pl.BlockSpec(memory_space=pltpu.SMEM)
HBM = pl.BlockSpec(memory_space=pltpu.HBM)
LIMIT = pltpu.CompilerParams(vmem_limit_bytes=24 * 1024 * 1024)


def far(array):
    return pltpu.with_memory_space_constraint(array, pltpu.HBM)
NT = (((1,), (1,)), ((), ()))
TN = (((0,), (0,)), ((), ()))


def halves(value):
    top = value.astype(BF16)
    return top, (value - top.astype(F32)).astype(BF16)


def slots_of(row):
    slots = row.shape[1]
    owner = row >> 6
    column = jnp.broadcast_to(owner.astype(F32), (128, slots)).T[:, 0:1]
    before = lax.broadcasted_iota(jnp.int32, (slots, slots), 0) < lax.broadcasted_iota(jnp.int32, (slots, slots), 1)
    same = (column == owner.astype(F32)) & before
    rank = jnp.sum(same.astype(F32), axis=0, keepdims=True)
    offset = (row & 63).astype(F32)
    owners = [jnp.where(rank == float(j), owner.astype(F32), -1.0) for j in range(SLOTS)]
    return jnp.concatenate(owners + [jnp.where(rank == float(j), offset, 0.0) for j in range(SLOTS)], axis=0)


def source_kernel(
    count_ref, obs_hbm, wt_hbm, js_hbm, ap_hbm, seg_hbm,
    sums_ref, upd_ref, resid_ref,
    obs_ref, wt_ref, js_ref, ap_ref, seg_ref, terms, sems,
):
    pairs = ((obs_hbm, obs_ref), (wt_hbm, wt_ref), (js_hbm, js_ref), (ap_hbm, ap_ref), (seg_hbm, seg_ref))
    copies = [pltpu.make_async_copy(src, dst, sems.at[i]) for i, (src, dst) in enumerate(pairs)]
    for copy in copies:
        copy.start()
    for copy in copies[0:3]:
        copy.wait()
    rows, slots = obs_ref.shape
    lane = lax.broadcasted_iota(jnp.int32, (1, slots), 1)
    used = (lane < count_ref[0]).astype(F32)
    live = wt_ref[...] * used
    obs = obs_ref[...]
    weighted = live * obs
    resid = obs
    for k in range(5):
        jac = js_ref[k]
        numer = jnp.sum(jac * weighted, axis=0, keepdims=True)
        denom = 1.0 + jnp.sum(jac * jac * live, axis=0, keepdims=True)
        update = numer / denom
        upd_ref[k : k + 1, :] = update
        resid = resid - jac * update
    resid_ref[...] = resid
    copies[3].wait()
    copies[4].wait()
    live_resid = live * resid
    for k in range(4):
        part = ap_ref[k]
        grad = part * live_resid
        diag = part * part * live
        for c in range(slots // 128):
            terms[c, pl.ds(k, rows, stride=8), :] = grad[:, 128 * c : 128 * c + 128]
            terms[c, pl.ds(4 + k, rows, stride=8), :] = diag[:, 128 * c : 128 * c + 128]
    ids = lax.broadcasted_iota(jnp.int32, (16, slots), 0).astype(F32).astype(BF16)
    left, right = [], []
    for r in range(rows):
        seg = seg_ref[r : r + 1, :]
        high = jnp.broadcast_to((seg >> 7).astype(F32), (16, slots)).astype(BF16)
        low = jnp.broadcast_to((seg & 127).astype(F32), (16, slots)).astype(BF16)
        value = jnp.concatenate([terms[c, 8 * r : 8 * r + 8, :] for c in range(slots // 128)], axis=1)
        top = value.astype(BF16).astype(F32)
        both = jnp.concatenate([value, value - top], axis=0).astype(BF16)
        zero = jnp.zeros_like(both)
        one = jnp.ones_like(both)
        left.append(jnp.concatenate([jnp.where(high == jnp.asarray(h, BF16), both, zero) for h in range(8)], axis=0))
        right.append(jnp.concatenate([jnp.where(low == ids + jnp.asarray(16 * g, BF16), one, zero) for g in range(8)], axis=0))
    total = lax.dot_general(jnp.concatenate(left, axis=1), jnp.concatenate(right, axis=1), NT, preferred_element_type=F32)
    for h in range(8):
        sums_ref[8 * h : 8 * h + 8, :] = total[16 * h : 16 * h + 8] + total[16 * h + 8 : 16 * h + 16]


def pick_rows(code_ref, j, owners):
    slots = code_ref.shape[1]
    ids = lax.broadcasted_iota(jnp.int32, (owners, slots), 0).astype(F32).astype(BF16)
    code = jnp.broadcast_to(code_ref[j : j + 1, :], (owners, slots)).astype(BF16)
    return jnp.where(ids == code, jnp.ones_like(code), jnp.zeros_like(code))


def near_kernel(
    count_ref, cal_hbm, wt_hbm, ap_hbm, seg_hbm, jac_hbm, live_ref, ap_ref, seg_ref, jac_ref, code_ref, send_ref, cal_ref, terms, sems
):
    rows, slots = live_ref.shape
    step = rows // 4
    pairs = [(cal_hbm, cal_ref), (wt_hbm, live_ref)]
    pairs += [(jac_hbm.at[pl.ds(step * q, step)], jac_ref.at[pl.ds(step * q, step)]) for q in range(4)]
    pairs += [(ap_hbm, ap_ref), (seg_hbm, seg_ref)]
    copies = [pltpu.make_async_copy(src, dst, sems.at[i]) for i, (src, dst) in enumerate(pairs)]
    for copy in copies:
        copy.start()
    copies[0].wait()
    code_ref[...] = slots_of(cal_ref[...])
    copies[1].wait()
    lane = lax.broadcasted_iota(jnp.int32, (1, slots), 1)
    live_ref[...] = live_ref[...] * (lane < count_ref[0]).astype(F32)
    for q in range(4):
        copies[2 + q].wait()
        for c in range(slots // 128):
            lanes = slice(128 * c, 128 * c + 128)
            diag = jnp.zeros((CPAR, 128), F32) if q == 0 else terms[:, lanes]
            for r in range(step * q, step * q + step):
                jac = jac_ref[r, :, lanes].astype(F32)
                diag = diag + jac * jac * live_ref[r : r + 1, lanes]
            terms[:, lanes] = diag
    top, rest = halves(terms[...])
    blank = jnp.zeros_like(top)
    both = jnp.concatenate([blank, top, blank, rest], axis=0)
    owners = send_ref.shape[0] // (SLOTS + 1)
    anywhere = jnp.zeros((owners, slots), BF16)
    for j in range(SLOTS):
        pick = pick_rows(code_ref, j, owners)
        anywhere = anywhere + pick
        moved = lax.dot_general(pick, both, NT, preferred_element_type=F32)
        send_ref[pl.ds(j, owners, stride=SLOTS + 1), :] = moved[:, 0:128] + moved[:, 128:256]
    offsets = jnp.concatenate([code_ref[SLOTS : 2 * SLOTS, :], jnp.zeros((128 - SLOTS, slots), F32)], axis=0).astype(BF16)
    moved = lax.dot_general(anywhere, offsets, NT, preferred_element_type=F32)
    send_ref[pl.ds(SLOTS, owners, stride=SLOTS + 1), :] = moved
    for copy in copies[6:]:
        copy.wait()


def residual_kernel(
    sums_ref, live_ref, ap_ref, seg_ref, jac_ref, resid_ref, code_ref, early_ref, att_ref, out_ref, send_ref, vec_buf, terms
):
    rows, slots = live_ref.shape
    tables = []
    for h in range(8):
        tile = sums_ref[8 * h : 8 * h + 8, :]
        tables.append(tile[0:4] / (1.0 + tile[4:8]))
    place = lax.axis_index("mem")
    tile = sums_ref[pl.ds(pl.multiple_of((place // 2) * 8, 8), 8), :]
    mine = tile[0:4] / (1.0 + tile[4:8])
    att_ref[...] = jnp.where(lax.rem(place, 2) == 0, mine[:, 0:64], mine[:, 64:128])

    for i in range(rows // 8):
        block = slice(8 * i, 8 * i + 8)
        for c in range(slots // 128):
            lanes = slice(128 * c, 128 * c + 128)
            seg = seg_ref[block, lanes]
            low = seg & 127
            bits = [(seg & (128 << n)) != 0 for n in range(3)]
            new = resid_ref[block, lanes]
            for k in range(4):
                found = [jnp.take_along_axis(jnp.broadcast_to(table[k : k + 1, :], (8, 128)), low, axis=1) for table in tables]
                for bit in bits:
                    found = [jnp.where(bit, odd, even) for even, odd in zip(found[0::2], found[1::2])]
                new = new - ap_ref[k, block, lanes] * found[0]
            out_ref[block, lanes] = new
            vec_buf[block, lanes] = new * live_ref[block, lanes]
    for c in range(slots // 128):
        lanes = slice(128 * c, 128 * c + 128)

        grad = jnp.zeros((CPAR, 128), F32)
        for r in range(rows):
            grad = grad + jac_ref[r, :, lanes].astype(F32) * vec_buf[r : r + 1, lanes]
        terms[:, lanes] = grad
    top, rest = halves(terms[...])
    blank = jnp.zeros_like(top)
    both = jnp.concatenate([top, blank, rest, blank], axis=0)
    owners = send_ref.shape[0] // (SLOTS + 1)
    for j in range(SLOTS):
        moved = lax.dot_general(pick_rows(code_ref, j, owners), both, NT, preferred_element_type=F32)
        part = pl.ds(j, owners, stride=SLOTS + 1)
        send_ref[part, :] = early_ref[part, :] + moved[:, 0:128] + moved[:, 128:256]
    part = pl.ds(SLOTS, owners, stride=SLOTS + 1)
    send_ref[part, :] = early_ref[part, :]


def gather_kernel(got_ref, out_ref):
    devices = got_ref.shape[0] // (SLOTS + 1)
    ids = lax.broadcasted_iota(jnp.int32, (devices, 64), 1).astype(F32)
    offsets = got_ref[pl.ds(SLOTS, devices, stride=SLOTS + 1), :]
    picks, parts = [], []
    for j in range(SLOTS):
        picks.append((ids == offsets[:, j : j + 1]).astype(F32).astype(BF16))
        parts.append(jnp.concatenate(halves(got_ref[pl.ds(j, devices, stride=SLOTS + 1), :]), axis=1))
    total = lax.dot_general(jnp.concatenate(picks, axis=0), jnp.concatenate(parts, axis=0), TN, preferred_element_type=F32)
    sums = total[:, 0:128] + total[:, 128:256]
    out_ref[...] = sums[:, 0:CPAR] / (1.0 + sums[:, CPAR : 2 * CPAR])


def step_pairs(core, x, y, z):
    pairs = []
    for i in range(256):
        grp, mem = divmod(i, 16)
        c, px, py, pz = mem & 1, (mem >> 1) & 3, ((mem >> 3) << 1) | (grp >> 3), grp & 7
        c, px, py, pz = c ^ core, px ^ x, py ^ y, pz ^ z
        pairs.append((i, ((py & 1) * 8 + pz) * 16 + (py >> 1) * 8 + px * 2 + c))
    return pairs


def moved(value, *step):
    return lax.ppermute(value, AXES, step_pairs(*step))


def body(obs_resid, weight, jac_src, att_part, seg_index, jac_cal, cal_index, block_count):
    slots = obs_resid.shape[0]
    devices = lax.axis_size(AXES)
    obs, wt, seg = far(obs_resid.T), far(weight.T), far(seg_index.T)
    js, ap = far(jac_src.transpose(0, 2, 1)), far(att_part.transpose(0, 2, 1))
    jac = far(jac_cal.transpose(1, 2, 0))
    plane = pltpu.VMEM((OBS, slots), F32)
    rows = pltpu.VMEM((devices * (SLOTS + 1), 128), F32)
    sums, src_update, resid_one = pl.pallas_call(
        source_kernel,
        out_shape=(pltpu.VMEM((64, 128), F32), jax.ShapeDtypeStruct((5, slots), F32), plane),
        in_specs=[SMEM] + [HBM] * 5,
        out_specs=(VMEM,) * 3,
        scratch_shapes=[
            pltpu.VMEM((OBS, slots), F32),
            pltpu.VMEM((OBS, slots), F32),
            pltpu.VMEM((5, OBS, slots), F32),
            pltpu.VMEM((4, OBS, slots), F32),
            pltpu.VMEM((OBS, slots), jnp.int32),
            pltpu.VMEM((slots // 128, OBS * 8, 128), F32),
            pltpu.SemaphoreType.DMA((5,)),
        ],
        compiler_params=LIMIT,
        name="source_step",
    )(block_count, obs, wt, js, ap, seg)
    live, near_ap, near_seg, near_jac, code, early = pl.pallas_call(
        near_kernel,
        out_shape=(
            plane,
            pltpu.VMEM((4, OBS, slots), F32),
            pltpu.VMEM((OBS, slots), jnp.int32),
            pltpu.VMEM((OBS, CPAR, slots), BF16),
            pltpu.VMEM((2 * SLOTS, slots), F32),
            rows,
        ),
        in_specs=[SMEM] + [HBM] * 5,
        out_specs=(VMEM,) * 6,
        scratch_shapes=[pltpu.VMEM((1, slots), jnp.int32), pltpu.VMEM((CPAR, slots), F32), pltpu.SemaphoreType.DMA((8,))],
        compiler_params=LIMIT,
        name="near_step",
    )(block_count, far(cal_index[None, :]), wt, ap, seg, jac)
    total = sums
    total = (total + moved(total, 0, 1, 0, 0)) + (moved(total, 0, 2, 0, 0) + moved(total, 0, 3, 0, 0))
    total = (total + moved(total, 0, 0, 1, 0)) + (moved(total, 0, 0, 2, 0) + moved(total, 0, 0, 3, 0))
    total = (total + moved(total, 0, 0, 0, 1)) + (moved(total, 0, 0, 0, 6) + moved(total, 0, 0, 0, 7))
    total, code = lax.optimization_barrier((total, code))
    total = (total + moved(total, 1, 0, 0, 0)) + (moved(total, 0, 0, 0, 2) + moved(total, 1, 0, 0, 2))
    att_out, new_resid, send = pl.pallas_call(
        residual_kernel,
        out_shape=(
            jax.ShapeDtypeStruct((4, KNOTS // lax.axis_size("mem")), F32),
            jax.ShapeDtypeStruct((OBS, slots), F32),
            rows,
        ),
        in_specs=[VMEM] * 8,
        out_specs=(VMEM,) * 3,
        scratch_shapes=[pltpu.VMEM((OBS, slots), F32), pltpu.VMEM((CPAR, slots), F32)],
        compiler_params=LIMIT,
        name="residual_step",
    )(total, live, near_ap, near_seg, near_jac, resid_one, code, early)
    got = lax.all_to_all(send.reshape(devices, 1, -1), AXES, 0, 0, tiled=True)
    cal_update = pl.pallas_call(
        gather_kernel,
        out_shape=jax.ShapeDtypeStruct((CALB // devices, CPAR), F32),
        in_specs=[VMEM],
        out_specs=VMEM,
        compiler_params=LIMIT,
        name="calibration_step",
    )(got.reshape(rows.shape))
    return src_update, att_out, cal_update, new_resid.T


def solution(mesh):
    return jax.shard_map(
        body,
        mesh=mesh,
        in_specs=(
            P(AXES, None),
            P(AXES, None),
            P(None, AXES, None),
            P(None, AXES, None),
            P(AXES, None),
            P(AXES, None, None),
            P(AXES),
            P(AXES),
        ),
        out_specs=(P(None, AXES), P(None, "mem"), P(AXES, None), P(AXES, None)),
        check_vma=False,
    )
```

```python
import jax
import jax.numpy as jnp
from jax import lax
from jax.experimental import pallas as pl
from jax.experimental.pallas import tpu as pltpu
from jax.sharding import PartitionSpec as P

CALB = 16384
CPAR = 64
KNOTS = 1024
OBS = 64
SLOTS = 4
AXES = ("grp", "mem")
F32 = jnp.float32
BF16 = jnp.bfloat16
VMEM = pl.BlockSpec(memory_space=pltpu.VMEM)
SMEM = pl.BlockSpec(memory_space=pltpu.SMEM)
HBM = pl.BlockSpec(memory_space=pltpu.HBM)
LIMIT = pltpu.CompilerParams(vmem_limit_bytes=24 * 1024 * 1024)


def far(array):
    return pltpu.with_memory_space_constraint(array, pltpu.HBM)
NT = (((1,), (1,)), ((), ()))
TN = (((0,), (0,)), ((), ()))


def halves(value):
    top = value.astype(BF16)
    return top, (value - top.astype(F32)).astype(BF16)


def slots_of(row):
    slots = row.shape[1]
    owner = row >> 6
    column = jnp.broadcast_to(owner.astype(F32), (128, slots)).T[:, 0:1]
    before = lax.broadcasted_iota(jnp.int32, (slots, slots), 0) < lax.broadcasted_iota(jnp.int32, (slots, slots), 1)
    same = (column == owner.astype(F32)) & before
    rank = jnp.sum(same.astype(F32), axis=0, keepdims=True)
    offset = (row & 63).astype(F32)
    owners = [jnp.where(rank == float(j), owner.astype(F32), -1.0) for j in range(SLOTS)]
    return jnp.concatenate(owners + [jnp.where(rank == float(j), offset, 0.0) for j in range(SLOTS)], axis=0)


def source_kernel(
    count_ref, obs_hbm, wt_hbm, js_hbm, ap_hbm, seg_hbm,
    sums_ref, upd_ref, resid_ref,
    obs_ref, wt_ref, js_ref, ap_ref, seg_ref, terms, sems,
):
    pairs = ((obs_hbm, obs_ref), (wt_hbm, wt_ref), (js_hbm, js_ref), (ap_hbm, ap_ref), (seg_hbm, seg_ref))
    copies = [pltpu.make_async_copy(src, dst, sems.at[i]) for i, (src, dst) in enumerate(pairs)]
    for copy in copies:
        copy.start()
    for copy in copies[0:3]:
        copy.wait()
    rows, slots = obs_ref.shape
    lane = lax.broadcasted_iota(jnp.int32, (1, slots), 1)
    used = (lane < count_ref[0]).astype(F32)
    live = wt_ref[...] * used
    obs = obs_ref[...]
    weighted = live * obs
    resid = obs
    for k in range(5):
        jac = js_ref[k]
        numer = jnp.sum(jac * weighted, axis=0, keepdims=True)
        denom = 1.0 + jnp.sum(jac * jac * live, axis=0, keepdims=True)
        update = numer / denom
        upd_ref[k : k + 1, :] = update
        resid = resid - jac * update
    resid_ref[...] = resid
    copies[3].wait()
    copies[4].wait()
    live_resid = live * resid
    for k in range(4):
        part = ap_ref[k]
        grad = part * live_resid
        diag = part * part * live
        for c in range(slots // 128):
            terms[c, pl.ds(k, rows, stride=8), :] = grad[:, 128 * c : 128 * c + 128]
            terms[c, pl.ds(4 + k, rows, stride=8), :] = diag[:, 128 * c : 128 * c + 128]
    ids = lax.broadcasted_iota(jnp.int32, (16, slots), 0).astype(F32).astype(BF16)
    left, right = [], []
    for r in range(rows):
        seg = seg_ref[r : r + 1, :]
        high = jnp.broadcast_to((seg >> 7).astype(F32), (16, slots)).astype(BF16)
        low = jnp.broadcast_to((seg & 127).astype(F32), (16, slots)).astype(BF16)
        value = jnp.concatenate([terms[c, 8 * r : 8 * r + 8, :] for c in range(slots // 128)], axis=1)
        top = value.astype(BF16).astype(F32)
        both = jnp.concatenate([value, value - top], axis=0).astype(BF16)
        zero = jnp.zeros_like(both)
        one = jnp.ones_like(both)
        left.append(jnp.concatenate([jnp.where(high == jnp.asarray(h, BF16), both, zero) for h in range(8)], axis=0))
        right.append(jnp.concatenate([jnp.where(low == ids + jnp.asarray(16 * g, BF16), one, zero) for g in range(8)], axis=0))
    total = lax.dot_general(jnp.concatenate(left, axis=1), jnp.concatenate(right, axis=1), NT, preferred_element_type=F32)
    for h in range(8):
        sums_ref[8 * h : 8 * h + 8, :] = total[16 * h : 16 * h + 8] + total[16 * h + 8 : 16 * h + 16]


def pick_rows(code_ref, j, owners):
    slots = code_ref.shape[1]
    ids = lax.broadcasted_iota(jnp.int32, (owners, slots), 0).astype(F32).astype(BF16)
    code = jnp.broadcast_to(code_ref[j : j + 1, :], (owners, slots)).astype(BF16)
    return jnp.where(ids == code, jnp.ones_like(code), jnp.zeros_like(code))


def near_kernel(
    count_ref, cal_hbm, wt_hbm, ap_hbm, seg_hbm, jac_hbm, live_ref, ap_ref, seg_ref, jac_ref, code_ref, send_ref, cal_ref, terms, sems
):
    rows, slots = live_ref.shape
    step = rows // 4
    pairs = [(cal_hbm, cal_ref), (wt_hbm, live_ref)]
    pairs += [(jac_hbm.at[pl.ds(step * q, step)], jac_ref.at[pl.ds(step * q, step)]) for q in range(4)]
    pairs += [(ap_hbm, ap_ref), (seg_hbm, seg_ref)]
    copies = [pltpu.make_async_copy(src, dst, sems.at[i]) for i, (src, dst) in enumerate(pairs)]
    for copy in copies:
        copy.start()
    copies[0].wait()
    code_ref[...] = slots_of(cal_ref[...])
    copies[1].wait()
    lane = lax.broadcasted_iota(jnp.int32, (1, slots), 1)
    live_ref[...] = live_ref[...] * (lane < count_ref[0]).astype(F32)
    for q in range(4):
        copies[2 + q].wait()
        for c in range(slots // 128):
            lanes = slice(128 * c, 128 * c + 128)
            diag = jnp.zeros((CPAR, 128), F32) if q == 0 else terms[:, lanes]
            for r in range(step * q, step * q + step):
                jac = jac_ref[r, :, lanes].astype(F32)
                diag = diag + jac * jac * live_ref[r : r + 1, lanes]
            terms[:, lanes] = diag
    top, rest = halves(terms[...])
    blank = jnp.zeros_like(top)
    both = jnp.concatenate([blank, top, blank, rest], axis=0)
    owners = send_ref.shape[0] // (SLOTS + 1)
    anywhere = jnp.zeros((owners, slots), BF16)
    for j in range(SLOTS):
        pick = pick_rows(code_ref, j, owners)
        anywhere = anywhere + pick
        moved = lax.dot_general(pick, both, NT, preferred_element_type=F32)
        send_ref[pl.ds(j, owners, stride=SLOTS + 1), :] = moved[:, 0:128] + moved[:, 128:256]
    offsets = jnp.concatenate([code_ref[SLOTS : 2 * SLOTS, :], jnp.zeros((128 - SLOTS, slots), F32)], axis=0).astype(BF16)
    moved = lax.dot_general(anywhere, offsets, NT, preferred_element_type=F32)
    send_ref[pl.ds(SLOTS, owners, stride=SLOTS + 1), :] = moved
    for copy in copies[6:]:
        copy.wait()


def residual_kernel(
    sums_ref, live_ref, ap_ref, seg_ref, jac_ref, resid_ref, code_ref, early_ref, att_ref, out_ref, send_ref, vec_buf, terms
):
    rows, slots = live_ref.shape
    tables = []
    for h in range(8):
        tile = sums_ref[8 * h : 8 * h + 8, :]
        tables.append(tile[0:4] / (1.0 + tile[4:8]))
    place = lax.axis_index("mem")
    tile = sums_ref[pl.ds(pl.multiple_of((place // 2) * 8, 8), 8), :]
    mine = tile[0:4] / (1.0 + tile[4:8])
    att_ref[...] = jnp.where(lax.rem(place, 2) == 0, mine[:, 0:64], mine[:, 64:128])

    for i in range(rows // 8):
        block = slice(8 * i, 8 * i + 8)
        for c in range(slots // 128):
            lanes = slice(128 * c, 128 * c + 128)
            seg = seg_ref[block, lanes]
            low = seg & 127
            bits = [(seg & (128 << n)) != 0 for n in range(3)]
            new = resid_ref[block, lanes]
            for k in range(4):
                found = [jnp.take_along_axis(jnp.broadcast_to(table[k : k + 1, :], (8, 128)), low, axis=1) for table in tables]
                for bit in bits:
                    found = [jnp.where(bit, odd, even) for even, odd in zip(found[0::2], found[1::2])]
                new = new - ap_ref[k, block, lanes] * found[0]
            out_ref[block, lanes] = new
            vec_buf[block, lanes] = new * live_ref[block, lanes]
    for c in range(slots // 128):
        lanes = slice(128 * c, 128 * c + 128)

        grad = jnp.zeros((CPAR, 128), F32)
        for r in range(rows):
            grad = grad + jac_ref[r, :, lanes].astype(F32) * vec_buf[r : r + 1, lanes]
        terms[:, lanes] = grad
    top, rest = halves(terms[...])
    blank = jnp.zeros_like(top)
    both = jnp.concatenate([top, blank, rest, blank], axis=0)
    owners = send_ref.shape[0] // (SLOTS + 1)
    for j in range(SLOTS):
        moved = lax.dot_general(pick_rows(code_ref, j, owners), both, NT, preferred_element_type=F32)
        part = pl.ds(j, owners, stride=SLOTS + 1)
        send_ref[part, :] = early_ref[part, :] + moved[:, 0:128] + moved[:, 128:256]
    part = pl.ds(SLOTS, owners, stride=SLOTS + 1)
    send_ref[part, :] = early_ref[part, :]


def gather_kernel(got_ref, out_ref):
    devices = got_ref.shape[0] // (SLOTS + 1)
    ids = lax.broadcasted_iota(jnp.int32, (devices, 64), 1).astype(F32)
    offsets = got_ref[pl.ds(SLOTS, devices, stride=SLOTS + 1), :]
    picks, parts = [], []
    for j in range(SLOTS):
        picks.append((ids == offsets[:, j : j + 1]).astype(F32).astype(BF16))
        parts.append(jnp.concatenate(halves(got_ref[pl.ds(j, devices, stride=SLOTS + 1), :]), axis=1))
    total = lax.dot_general(jnp.concatenate(picks, axis=0), jnp.concatenate(parts, axis=0), TN, preferred_element_type=F32)
    sums = total[:, 0:128] + total[:, 128:256]
    out_ref[...] = sums[:, 0:CPAR] / (1.0 + sums[:, CPAR : 2 * CPAR])


def step_pairs(core, x, y, z):
    pairs = []
    for i in range(256):
        grp, mem = divmod(i, 16)
        c, px, py, pz = mem & 1, (mem >> 1) & 3, ((mem >> 3) << 1) | (grp >> 3), grp & 7
        c, px, py, pz = c ^ core, px ^ x, py ^ y, pz ^ z
        pairs.append((i, ((py & 1) * 8 + pz) * 16 + (py >> 1) * 8 + px * 2 + c))
    return pairs


def moved(value, *step):
    return lax.ppermute(value, AXES, step_pairs(*step))


def body(obs_resid, weight, jac_src, att_part, seg_index, jac_cal, cal_index, block_count):
    slots = obs_resid.shape[0]
    devices = lax.axis_size(AXES)
    obs, wt, seg = far(obs_resid.T), far(weight.T), far(seg_index.T)
    js, ap = far(jac_src.transpose(0, 2, 1)), far(att_part.transpose(0, 2, 1))
    jac = far(jac_cal.transpose(1, 2, 0))
    plane = pltpu.VMEM((OBS, slots), F32)
    rows = pltpu.VMEM((devices * (SLOTS + 1), 128), F32)
    sums, src_update, resid_one = pl.pallas_call(
        source_kernel,
        out_shape=(pltpu.VMEM((64, 128), F32), jax.ShapeDtypeStruct((5, slots), F32), plane),
        in_specs=[SMEM] + [HBM] * 5,
        out_specs=(VMEM,) * 3,
        scratch_shapes=[
            pltpu.VMEM((OBS, slots), F32),
            pltpu.VMEM((OBS, slots), F32),
            pltpu.VMEM((5, OBS, slots), F32),
            pltpu.VMEM((4, OBS, slots), F32),
            pltpu.VMEM((OBS, slots), jnp.int32),
            pltpu.VMEM((slots // 128, OBS * 8, 128), F32),
            pltpu.SemaphoreType.DMA((5,)),
        ],
        compiler_params=LIMIT,
        name="source_step",
    )(block_count, obs, wt, js, ap, seg)
    live, near_ap, near_seg, near_jac, code, early = pl.pallas_call(
        near_kernel,
        out_shape=(
            plane,
            pltpu.VMEM((4, OBS, slots), F32),
            pltpu.VMEM((OBS, slots), jnp.int32),
            pltpu.VMEM((OBS, CPAR, slots), BF16),
            pltpu.VMEM((2 * SLOTS, slots), F32),
            rows,
        ),
        in_specs=[SMEM] + [HBM] * 5,
        out_specs=(VMEM,) * 6,
        scratch_shapes=[pltpu.VMEM((1, slots), jnp.int32), pltpu.VMEM((CPAR, slots), F32), pltpu.SemaphoreType.DMA((8,))],
        compiler_params=LIMIT,
        name="near_step",
    )(block_count, far(cal_index[None, :]), wt, ap, seg, jac)
    total = sums
    total = (total + moved(total, 1, 0, 0, 0)) + (moved(total, 0, 0, 0, 1) + moved(total, 1, 0, 0, 1))
    total = (total + moved(total, 0, 1, 0, 0)) + (moved(total, 0, 2, 0, 0) + moved(total, 0, 3, 0, 0))
    total = (total + moved(total, 0, 0, 1, 0)) + (moved(total, 0, 0, 2, 0) + moved(total, 0, 0, 3, 0))
    total, code = lax.optimization_barrier((total, code))
    total = (total + moved(total, 0, 0, 0, 2)) + (moved(total, 0, 0, 0, 4) + moved(total, 0, 0, 0, 6))
    att_out, new_resid, send = pl.pallas_call(
        residual_kernel,
        out_shape=(
            jax.ShapeDtypeStruct((4, KNOTS // lax.axis_size("mem")), F32),
            jax.ShapeDtypeStruct((OBS, slots), F32),
            rows,
        ),
        in_specs=[VMEM] * 8,
        out_specs=(VMEM,) * 3,
        scratch_shapes=[pltpu.VMEM((OBS, slots), F32), pltpu.VMEM((CPAR, slots), F32)],
        compiler_params=LIMIT,
        name="residual_step",
    )(total, live, near_ap, near_seg, near_jac, resid_one, code, early)
    got = lax.all_to_all(send.reshape(devices, 1, -1), AXES, 0, 0, tiled=True)
    cal_update = pl.pallas_call(
        gather_kernel,
        out_shape=jax.ShapeDtypeStruct((CALB // devices, CPAR), F32),
        in_specs=[VMEM],
        out_specs=VMEM,
        compiler_params=LIMIT,
        name="calibration_step",
    )(got.reshape(rows.shape))
    return src_update, att_out, cal_update, new_resid.T


def solution(mesh):
    return jax.shard_map(
        body,
        mesh=mesh,
        in_specs=(
            P(AXES, None),
            P(AXES, None),
            P(None, AXES, None),
            P(None, AXES, None),
            P(AXES, None),
            P(AXES, None, None),
            P(AXES),
            P(AXES),
        ),
        out_specs=(P(None, AXES), P(None, "mem"), P(AXES, None), P(AXES, None)),
        check_vma=False,
    )
```
